256 devices in a mesh: dp: 32 (over y_hi, z, core), expert: 8 (over x, y_lo).
Axes of the slice: x: 4, y: 4 (y_hi: 2, y_lo: 2; y = y_hi * 2 + y_lo), z: 8, core: 2. Of those that a mesh axis runs over, the one named last changes fastest.
Arguments:
- tokens: float32 [32768, 3584], P(('dp', 'expert')), may hold values from -24 to 24
- cotangent: float32 [32768, 3584], P(('dp', 'expert')), may hold values from -6 to 6
- routes: int32 [32768, 2], P(('dp', 'expert')), may hold values from 0 to 7, all different within a row; in each aligned block of 128 rows (0 to 127, 128 to 255, ...) at most 40 rows name the same one
- gates: float32 [32768, 2], P(('dp', 'expert')), may hold values from 0.1 to 1
- w_gate: float32 [8, 3584, 128], P('expert', 'dp'), may hold values from -0.09375 to 0.09375
- w_up: float32 [8, 3584, 128], P('expert', 'dp'), may hold values from -0.09375 to 0.09375
- w_down: float32 [8, 3584, 128], P('expert', 'dp'), may hold values from -0.5 to 0.5
Outputs:
- grad_tokens: float32 [32768, 3584], P(('dp', 'expert'))
- grad_gate: float32 [8, 3584, 128], P('expert', 'dp')
- grad_up: float32 [8, 3584, 128], P('expert', 'dp')
- grad_down: float32 [8, 3584, 128], P('expert', 'dp')
The draws below stay inside these ranges and needn't reach their ends.
Inputs may be any that keep to these rules, and one draw needn't show every extreme that they name: Within the rows of one device (aligned blocks of 128 rows), no expert is named by more than 40 routes, a bound that some block reaches; the 2 experts of a row differ.
All inputs are finite; a program needn't handle non-finite values.
Results may differ from the reference program's by a relative error of at most 0.0003.
Values sent between devices are 32-bit elements; how exact they have to be, the bound alone decides.
A program may use at most 128 MiB of HBM per device.

```python
import math
import jax
import jax.numpy as jnp
import numpy as np
from jax import lax

D = 3584
HID = 128
TOP = 2
TOK_DEV = 128
EXPERTS = 8
CAP = 40
TOKENS = 32768
N_DP = 32
N_EXPERT = 8


def with_spikes(result, stream_key, source, target, blocks, factor):
    def block_of(position):
        return (jnp.arange(result.shape[position]) // (result.shape[position] // blocks)).reshape((-1,) + (1,) * (result.ndim - 1 - position))

    one_side = jax.random.permutation(stream_key, blocks)[block_of(target)]
    second = (block_of(target) + blocks // 2) % blocks
    return jnp.where((block_of(source) == one_side) | (block_of(source) == second), factor * result, result)


def block_scale(key, dims, cuts, smallest, largest):
    level = 1.0
    for dim, blocks in cuts:
        steps = jax.random.uniform(jax.random.fold_in(jax.random.fold_in(key, 6), dim), (blocks,), jnp.float32, smallest / len(cuts), largest / len(cuts))
        level = level * jnp.repeat(jnp.exp(steps), dims[dim] // blocks).reshape((-1,) + (1,) * (len(dims) - 1 - dim))
    return level


def routed_block(stream_key, own, number, rows, amount, top, reach, slope):
    sequence = jax.random.permutation(stream_key, amount)
    heavy_load, common = shares(amount, rows * top, reach, slope, True), shares(amount, rows * top, reach, slope, False)
    places = jnp.arange(amount)

    def named(lengths, turn):
        used = int((lengths > 0).sum())
        fixed = max(1, used // 4)
        shifted = fixed + (places - fixed + turn * (used - fixed)) % max(1, amount - fixed)
        return jnp.zeros((amount,), jnp.int32).at[sequence[jnp.where(places < fixed, places, shifted)]].set(jnp.asarray(lengths, jnp.int32))

    lengths = jnp.where(number % 4 == 0, named(heavy_load, number // 4), named(common, number - number // 4 - 1))
    mixed = jax.random.permutation(jax.random.fold_in(own, 3), amount)
    giver, taker = mixed[0:amount // 2 * 2:2], mixed[1:amount // 2 * 2:2]
    margin = jnp.minimum(lengths[giver] - 1, reach - lengths[taker]) // 2
    margin = jnp.where((giver == sequence[0]) | (taker == sequence[0]) | (lengths[taker] == 0), 0, jnp.maximum(margin, 0))
    shifted = jax.random.randint(jax.random.fold_in(own, 4), (amount // 2,), 0, 1 << 20) % (margin + 1)
    lengths = lengths.at[giver].add(-shifted).at[taker].add(shifted)
    members = jnp.searchsorted(jnp.cumsum(lengths), jnp.arange(rows * top), side="right").astype(jnp.int32)
    listing = members.reshape(top, rows).T
    listing = listing[jax.random.permutation(jax.random.fold_in(own, 1), rows)]
    turn = jax.random.randint(jax.random.fold_in(own, 2), (rows, 1), 0, top)
    return jnp.take_along_axis(listing, (jnp.arange(top)[None, :] + turn) % top, axis=1)


def shares(count, total, bound, skew, full):
    loads = [(1 << 20) // math.isqrt(standing ** skew) + 1 for standing in range(1, count + 1)]
    largest = bound if full else min(bound, max(-(-total // count), total * loads[0] // sum(loads)))
    least = 1 if total - largest >= count - 1 else 0
    holding, rest = [largest] + [least] * (count - 1), total - largest - least * (count - 1)
    while rest > 0:
        movable = [i for i in range(1, count) if holding[i] < largest] or [i for i in range(1, count) if holding[i] < bound]
        pool, budget = sum([loads[i] for i in movable]), rest
        for i in movable:
            addition = min(bound - holding[i], max(1, budget * loads[i] // pool), rest)
            holding[i] = holding[i] + addition
            rest = rest - addition
    return np.array(holding)


def normal_values(key, dims, width, most, split=(), kind=jnp.bfloat16):
    loudness = block_scale(key, dims, split, -0.22, 0.18) if split else 1.0
    result = jax.random.normal(key, dims, jnp.float32) * width * loudness
    return jnp.minimum(jnp.maximum(result, -most), most).astype(kind)


def gaussian_with(stream_key, shape, deviation, most, pieces, heavy, held_as=jnp.bfloat16):
    entries = deviation * jax.random.normal(stream_key, shape, jnp.float32)
    if pieces:
        entries = entries * block_scale(stream_key, shape, pieces, -0.22, 0.18)
    return jnp.clip(with_spikes(entries, jax.random.fold_in(stream_key, 3), *heavy), -most, most).astype(held_as)


def setup_inputs(seed: int = 0) -> dict:
    splits = jax.random.split(jax.random.key(seed), 8)
    tokens = gaussian_with(splits[0], (TOKENS, D), 1.0, 24.0, ((0, 256),), (0, 1, 256, 6.0), jnp.float32)
    cotangent = normal_values(splits[1], (TOKENS, D), 1.0, 6.0, ((0, 256),), jnp.float32)
    routes_keys = jax.random.split(jax.random.fold_in(splits[2], 1), TOKENS // TOK_DEV)
    routes_turns = jax.random.permutation(jax.random.fold_in(splits[2], 3), TOKENS // TOK_DEV)
    routes = jax.vmap(lambda own, number: routed_block(jax.random.fold_in(splits[2], 2), own, number, TOK_DEV, EXPERTS, TOP, CAP, 2))(routes_keys, routes_turns).reshape((TOKENS, TOP))
    gates = jnp.clip(0.1 + 0.9 * jax.random.uniform(splits[3], (TOKENS, TOP), jnp.float32) ** block_scale(splits[3], (TOKENS, TOP), ((0, 256),), -0.2, 0.2), 0.1, 1.0)
    w_gate = normal_values(splits[4], (EXPERTS, D, HID), D ** -0.5, 0.09375, ((0, 8), (1, 32)), jnp.float32)
    w_up = normal_values(splits[5], (EXPERTS, D, HID), D ** -0.5, 0.09375, ((0, 8), (1, 32)), jnp.float32)
    w_down = normal_values(splits[6], (EXPERTS, D, HID), HID ** -0.5, 0.5, ((0, 8), (1, 32)), jnp.float32)
    return {"tokens": tokens, "cotangent": cotangent, "routes": routes, "gates": gates, "w_gate": w_gate, "w_up": w_up, "w_down": w_down}


highest = lax.Precision.HIGHEST


def silu_parts(pre_act):
    sigmoid_val = jax.nn.sigmoid(pre_act)
    return pre_act * sigmoid_val, sigmoid_val * (1.0 + pre_act * (1.0 - sigmoid_val))


def contract_rows(left_side, right_side):
    return lax.dot_general(left_side, right_side, (((0,), (0,)), ((), ())), precision=highest)


def contract_columns(left_side, right_side):
    return lax.dot_general(left_side, right_side, (((1,), (1,)), ((), ())), precision=highest)


def reference(tokens, cotangent, routes, gates, w_gate, w_up, w_down):
    top_count = routes.shape[1]
    limit = N_DP * N_EXPERT * CAP
    flat_expert = routes.reshape(-1)
    flat_gate = gates.reshape(-1)

    def per_expert(grad_tokens, element):
        expert_id, gate_block, up_block, down_block = element
        chosen = flat_expert == expert_id
        ordering = jnp.argsort(jnp.where(chosen, 0, 1).astype(jnp.int32), stable=True)[:limit].astype(jnp.int32)
        present = chosen[ordering][:, None]
        token_index = (ordering // top_count).astype(jnp.int32)
        picked_rows = jnp.where(present, tokens[token_index], 0.0)
        scaled = jnp.where(present, cotangent[token_index] * flat_gate[ordering][:, None], 0.0)
        pre_gate = jnp.dot(picked_rows, gate_block, precision=highest)
        pre_up = jnp.dot(picked_rows, up_block, precision=highest)
        back_hidden = jnp.dot(scaled, down_block, precision=highest)
        activated, slopes = silu_parts(pre_gate)
        hidden = activated * pre_up
        grad_gate_pre = back_hidden * pre_up * slopes
        grad_up_pre = back_hidden * activated
        row_grads = contract_columns(grad_gate_pre, gate_block) + contract_columns(grad_up_pre, up_block)
        grad_tokens = grad_tokens.at[token_index].add(jnp.where(present, row_grads, 0.0))
        return grad_tokens, (contract_rows(picked_rows, grad_gate_pre), contract_rows(picked_rows, grad_up_pre), contract_rows(scaled, hidden))

    start_grads = jnp.zeros(tokens.shape, jnp.float32)
    expert_ids = jnp.arange(EXPERTS, dtype=jnp.int32)
    grad_tokens, stacked = lax.scan(per_expert, start_grads, (expert_ids, w_gate, w_up, w_down))
    return grad_tokens, stacked[0], stacked[1], stacked[2]
```

```python
import functools

import jax
import jax.numpy as jnp
from jax import lax
from jax.experimental import pallas as pl
from jax.experimental.pallas import tpu as pltpu
from jax.sharding import PartitionSpec as P

MESH = pl.DeviceIdType.MESH
HIGH = lax.Precision.HIGH
VMEM_LIMIT = 60 * 2**20
ROWS = 112
TOK = 128
F32 = jnp.float32


def coords():
    dp = lax.axis_index("dp")
    e = lax.axis_index("expert")
    return e // 2, (dp // 16) * 2 + e % 2, (dp // 2) % 8, dp % 2


def dev(x, y, z, c):
    x, y, z, c = (x + 4) % 4, (y + 4) % 4, (z + 8) % 8, c % 2
    return ((y // 2) * 8 + z) * 2 + c, x * 2 + y % 2


def remote(src, dst, ss, rs, to):
    return pltpu.make_async_remote_copy(
        src_ref=src, dst_ref=dst, send_sem=ss, recv_sem=rs, device_id=to, device_id_type=MESH
    )


def greet(peers):
    bar = pltpu.get_barrier_semaphore()
    for p in peers:
        pl.semaphore_signal(bar, 1, device_id=p, device_id_type=MESH)
    pl.semaphore_wait(bar, len(peers))


OTHERS = [(dc, dy) for dy in (2, 1, 3, 0) for dc in (0, 1) if (dc, dy) != (0, 0)]


def gather_kernel(x_ref, w_ref, xg, wg, ss_x, rs_x, ss_p, rs_p, ss_z, rs_z, ss_r, rs_r, lsem):
    x, y, z, c = coords()
    yl = y % 2
    good = (z % 2) == yl
    me = c * 4 + y
    zi = z // 2
    zp, zm = dev(x, y, z + 1, c), dev(x, y, z - 1, c)
    xp, xm = dev(x + 1, y, z, c), dev(x - 1, y, z, c)
    partner = dev(x, (y // 2) * 2 + 1 - yl, z, c)
    greet([dev(x, y + dy, z, c + dc) for dc, dy in OTHERS] + [zp, zm, xp, xm])

    def blk(xx, b):
        return wg.at[:, pl.ds(((b + 4) % 4) * ROWS, ROWS), pl.ds(((xx + 4) % 4) * 256, 256)]

    def half(xx, b, h):
        return wg.at[:, pl.ds(((b + 4) % 4) * ROWS, ROWS), pl.ds(((xx + 4) % 4) * 256 + h * 128, 128)]

    own = half(x, zi, yl)
    local = pltpu.make_async_copy(w_ref, own, lsem.at[0])
    shift = remote(w_ref, own, ss_p, rs_p, partner)

    @pl.when(good)
    def _():
        local.start()

    @pl.when(jnp.logical_not(good))
    def _():
        shift.start()

    keep = pltpu.make_async_copy(x_ref.at[me], xg.at[me], lsem.at[1])
    keep.start()
    sends = []
    for i, (dc, dy) in enumerate(OTHERS):
        y2, c2 = (y + dy) % 4, (c + dc) % 2
        cp = remote(x_ref.at[c2 * 4 + y2], xg.at[me], ss_x.at[i], rs_x.at[i], dev(x, y2, z, c2))
        cp.start()
        sends.append(cp)

    def zsend(i, ref, to):
        return remote(ref, ref, ss_z.at[i], rs_z.at[i], to)

    def xsend(s, b):
        return (
            remote(blk(x, b), blk(x, b), ss_r.at[s, 0], rs_r.at[s, 0], xp),
            remote(blk(x, b), blk(x, b), ss_r.at[s, 1], rs_r.at[s, 1], xm),
        )

    def xfwd(s, b):
        return (
            remote(half(x - 1, b, 0), half(x - 1, b, 0), ss_r.at[s, 2], rs_r.at[s, 2], xp),
            remote(half(x + 1, b, 1), half(x + 1, b, 1), ss_r.at[s, 3], rs_r.at[s, 3], xm),
        )

    def recv_x(s, b):
        return (
            remote(blk(x - 1, b), blk(x - 1, b), ss_r.at[s, 0], rs_r.at[s, 0], xp),
            remote(blk(x + 1, b), blk(x + 1, b), ss_r.at[s, 1], rs_r.at[s, 1], xm),
        )

    def recv_f(s, b):
        return (
            remote(half(x - 2, b, 0), half(x - 2, b, 0), ss_r.at[s, 2], rs_r.at[s, 2], xp),
            remote(half(x + 2, b, 1), half(x + 2, b, 1), ss_r.at[s, 3], rs_r.at[s, 3], xm),
        )

    def start_x(s, b):
        for cp in xsend(s, b):
            cp.start()

    def forward_x(s, b):
        for got, cp in zip(recv_x(s, b), xfwd(s, b)):
            got.wait_recv()
            cp.start()

    def finish_x(s, b):
        for got in recv_f(s, b):
            got.wait_recv()
        for cp in xsend(s, b) + xfwd(s, b):
            cp.wait_send()

    @pl.when(good)
    def _():
        local.wait()
        remote(w_ref, half(x, zi, 1 - yl), ss_p, rs_p, partner).wait_recv()
        s1p, s1m = zsend(0, blk(x, zi), zp), zsend(2, blk(x, zi), zm)
        s1p.start()
        s1m.start()
        start_x(0, zi)
        forward_x(0, zi)
        zsend(0, blk(x, zi - 1), zp).wait_recv()
        s2p = zsend(1, blk(x, zi - 1), zp)
        s2p.start()
        start_x(1, zi - 1)
        zsend(2, blk(x, zi + 1), zm).wait_recv()
        s2m = zsend(3, blk(x, zi + 1), zm)
        s2m.start()
        start_x(2, zi + 1)
        forward_x(1, zi - 1)
        forward_x(2, zi + 1)
        zsend(1, half(x, zi - 2, 0), zp).wait_recv()
        zsend(3, half(x, zi + 2, 1), zm).wait_recv()
        start_x(3, zi + 2)
        forward_x(3, zi + 2)
        for s, b in ((0, zi), (1, zi - 1), (2, zi + 1), (3, zi + 2)):
            finish_x(s, b)
        for cp in (s1p, s1m, s2p, s2m):
            cp.wait_send()

    @pl.when(jnp.logical_not(good))
    def _():
        lo = (z - 1 - yl + 8) // 2
        hi = lo + 1
        zsend(0, blk(x, lo), zp).wait_recv()
        s1p = zsend(0, blk(x, lo), zp)
        s1p.start()
        start_x(0, lo)
        zsend(2, blk(x, hi), zm).wait_recv()
        s1m = zsend(2, blk(x, hi), zm)
        s1m.start()
        start_x(1, hi)
        forward_x(0, lo)
        forward_x(1, hi)
        zsend(1, blk(x, lo - 1), zp).wait_recv()
        s2p = zsend(1, half(x, lo - 1, 0), zp)
        s2p.start()
        start_x(2, lo - 1)
        zsend(3, blk(x, hi + 1), zm).wait_recv()
        s2m = zsend(3, half(x, hi + 1, 1), zm)
        s2m.start()
        start_x(3, hi + 1)
        forward_x(2, lo - 1)
        forward_x(3, hi + 1)
        for s, b in ((0, lo), (1, hi), (2, lo - 1), (3, hi + 1)):
            finish_x(s, b)
        for cp in (shift, s1p, s1m, s2p, s2m):
            cp.wait_send()

    for cp in sends:
        cp.wait()
    keep.wait()


def hidden_kernel(p_ref, gate_ref, ga, buf, got, ss, rs, ss_r, rs_r, ss_g, rs_g, ss_f, rs_f):
    x, y, z, c = coords()
    sib = dev(x, y, z, 1 - c)
    peers = [dev(x, y + dy, z, c) for dy in (2, 1, 3)]
    greet(peers + [sib])
    firsts = []
    for i, dy in enumerate((2, 1, 3, 0)):
        y2 = (y + dy) % 4
        cp = remote(p_ref.at[1 - c, y2], buf.at[y2], ss.at[i], rs.at[i], sib)
        cp.start()
        firsts.append(cp)
    seconds = []
    for i, dy in enumerate((2, 1, 3, 0)):
        y2 = (y + dy) % 4
        firsts[i].wait_recv()
        buf[y2] = buf[y2] + p_ref[c, y2]
        if dy:
            cp = remote(buf.at[y2], got.at[i], ss_r.at[i], rs_r.at[i], dev(x, y2, z, c))
            cp.start()
            seconds.append(cp)
    total = buf[y]
    for i in range(3):
        seconds[i].wait_recv()
        total = total + got[i]
    for k in range(2):
        gate = gate_ref[:, k * 128 : (k + 1) * 128]
        base = k * 384
        pre_gate = total[:, base : base + 128]
        pre_up = total[:, base + 128 : base + 256]
        back = total[:, base + 256 : base + 384] * gate
        s = jax.nn.sigmoid(pre_gate)
        activated = pre_gate * s
        slopes = s * (1.0 + pre_gate * (1.0 - s))
        ga[c, y, :, base : base + 128] = back * pre_up * slopes
        ga[c, y, :, base + 128 : base + 256] = back * activated
        ga[c, y, :, base + 256 : base + 384] = activated * pre_up * gate
    outs = []
    for i, dy in enumerate((2, 1, 3)):
        cp = remote(ga.at[c, y], ga.at[c, y], ss_g.at[i], rs_g.at[i], peers[i])
        cp.start()
        outs.append(cp)
    fw = [remote(ga.at[c, y], ga.at[c, y], ss_f.at[3], rs_f.at[3], sib)]
    fw[0].start()
    for i, dy in ((1, 1), (2, 3), (0, 2)):
        y2 = (y - dy + 4) % 4
        remote(ga.at[c, y2], ga.at[c, y2], ss_g.at[i], rs_g.at[i], peers[i]).wait_recv()
        cp = remote(ga.at[c, y2], ga.at[c, y2], ss_f.at[i], rs_f.at[i], sib)
        cp.start()
        fw.append(cp)
    for i, dy in ((3, 0), (1, 1), (2, 3), (0, 2)):
        y2 = (y - dy + 4) % 4
        remote(ga.at[1 - c, y2], ga.at[1 - c, y2], ss_f.at[i], rs_f.at[i], sib).wait_recv()
    for cp in firsts + seconds + outs + fw:
        cp.wait_send()


def scatter_kernel(
    gt_ref, gw_ref, gx, gout, acc, xh, xf, zh, z1, z2, z3, pbuf, zsnd,
    ss_x, rs_x, ss_p, rs_p, ss_z, rs_z, ss_r, rs_r, lsem,
):
    x, y, z, c = coords()
    yl = y % 2
    good = (z % 2) == yl
    me = c * 4 + y
    zi = z // 2
    zp, zm = dev(x, y, z + 1, c), dev(x, y, z - 1, c)
    xp, xm = dev(x + 1, y, z, c), dev(x - 1, y, z, c)
    partner = dev(x, (y // 2) * 2 + 1 - yl, z, c)
    greet([dev(x, y + dy, z, c + dc) for dc, dy in OTHERS] + [zp, zm, xp, xm])

    def rows(b):
        return pl.ds(((b + 4) % 4) * ROWS, ROWS)

    def cols(xx):
        return pl.ds(((xx + 4) % 4) * 256, 256)

    def hcols(xx, h):
        return pl.ds(((xx + 4) % 4) * 256 + h * 128, 128)

    def start_half(s, b):
        cps = (
            remote(gw_ref.at[:, rows(b), hcols(x + 2, 0)], xh.at[s, 0], ss_r.at[s, 0], rs_r.at[s, 0], xp),
            remote(gw_ref.at[:, rows(b), hcols(x + 2, 1)], xh.at[s, 1], ss_r.at[s, 1], rs_r.at[s, 1], xm),
        )
        for cp in cps:
            cp.start()
        return cps

    def start_full(s, b, halves):
        halves[0].wait_recv()
        acc[s, 0, :, :, 0:128] = gw_ref[:, rows(b), hcols(x + 1, 0)] + xh[s, 0]
        acc[s, 0, :, :, 128:256] = gw_ref[:, rows(b), hcols(x + 1, 1)]
        up = remote(acc.at[s, 0], xf.at[s, 0], ss_r.at[s, 2], rs_r.at[s, 2], xp)
        up.start()
        halves[1].wait_recv()
        acc[s, 1, :, :, 0:128] = gw_ref[:, rows(b), hcols(x - 1, 0)]
        acc[s, 1, :, :, 128:256] = gw_ref[:, rows(b), hcols(x - 1, 1)] + xh[s, 1]
        down = remote(acc.at[s, 1], xf.at[s, 1], ss_r.at[s, 3], rs_r.at[s, 3], xm)
        down.start()
        return up, down

    def total(s, b, fulls):
        fulls[0].wait_recv()
        fulls[1].wait_recv()
        return gw_ref[:, rows(b), cols(x)] + xf[s, 0] + xf[s, 1]

    sends = []

    def start_return():
        for i, (dc, dy) in enumerate(OTHERS):
            y2, c2 = (y + dy) % 4, (c + dc) % 2
            cp = remote(gt_ref.at[c2 * 4 + y2], gx.at[me], ss_x.at[i], rs_x.at[i], dev(x, y2, z, c2))
            cp.start()
            sends.append(cp)

    keep = pltpu.make_async_copy(gt_ref.at[me], gx.at[me], lsem)
    keep.start()
    start_return()

    def run(order):
        halves = [start_half(s, b) for s, b in enumerate(order)]
        fulls = [start_full(s, b, halves[s]) for s, b in enumerate(order)]
        return halves, fulls

    def finish(halves, fulls):
        for pair in halves + fulls:
            for cp in pair:
                cp.wait_send()

    def zc(i, src, dst, to):
        return remote(src, dst, ss_z.at[i], rs_z.at[i], to)

    @pl.when(good)
    def _():
        order = (zi + 2, zi + 1, zi - 1, zi)
        halves, fulls = run(order)
        t = total(0, order[0], fulls[0])
        zsnd[0, :, :, 0:128] = t[:, :, 0:128]
        zsnd[1, :, :, 0:128] = t[:, :, 128:256]
        a = zc(0, zsnd.at[0, :, :, pl.ds(0, 128)], zh.at[0], zp)
        b = zc(2, zsnd.at[1, :, :, pl.ds(0, 128)], zh.at[1], zm)
        a.start()
        b.start()
        up = total(1, order[1], fulls[1])
        zc(0, zsnd.at[2], z1.at[0], zp).wait_recv()
        zsnd[2] = up + z1[0]
        a2 = zc(1, zsnd.at[2], z2.at[0], zp)
        a2.start()
        down = total(2, order[2], fulls[2])
        zc(2, zsnd.at[3], z1.at[1], zm).wait_recv()
        zsnd[3] = down + z1[1]
        b2 = zc(3, zsnd.at[3], z2.at[1], zm)
        b2.start()
        t = total(3, order[3], fulls[3])
        zc(1, zsnd.at[2], z3.at[0], zp).wait_recv()
        zc(3, zsnd.at[3], z3.at[1], zm).wait_recv()
        t = t + z3[0] + z3[1]
        pbuf[0] = t[:, :, 0:128]
        pbuf[1] = t[:, :, 128:256]
        shift = remote(pbuf.at[1 - yl], gout, ss_p, rs_p, partner)
        shift.start()
        gout[...] = pbuf[yl]
        for cp in (a, b, a2, b2, shift):
            cp.wait_send()
        finish(halves, fulls)

    @pl.when(jnp.logical_not(good))
    def _():
        lo = (z - 1 - yl + 8) // 2
        hi = lo + 1
        order = (hi + 1, lo - 1, hi, lo)
        halves, fulls = run(order)
        t = total(0, order[0], fulls[0])
        zc(0, zsnd.at[0, :, :, pl.ds(0, 128)], zh.at[0], zp).wait_recv()
        zsnd[0, :, :, 0:128] = t[:, :, 0:128] + zh[0]
        zsnd[0, :, :, 128:256] = t[:, :, 128:256]
        a = zc(0, zsnd.at[0], z1.at[0], zp)
        a.start()
        t = total(1, order[1], fulls[1])
        zc(2, zsnd.at[1, :, :, pl.ds(0, 128)], zh.at[1], zm).wait_recv()
        zsnd[1, :, :, 0:128] = t[:, :, 0:128]
        zsnd[1, :, :, 128:256] = t[:, :, 128:256] + zh[1]
        b = zc(2, zsnd.at[1], z1.at[1], zm)
        b.start()
        t = total(2, order[2], fulls[2])
        zc(1, zsnd.at[2], z2.at[0], zp).wait_recv()
        zsnd[2] = t + z2[0]
        a2 = zc(1, zsnd.at[2], z3.at[0], zp)
        a2.start()
        t = total(3, order[3], fulls[3])
        zc(3, zsnd.at[3], z2.at[1], zm).wait_recv()
        zsnd[3] = t + z2[1]
        b2 = zc(3, zsnd.at[3], z3.at[1], zm)
        b2.start()
        remote(pbuf.at[0], gout, ss_p, rs_p, partner).wait_recv()
        for cp in (a, b, a2, b2):
            cp.wait_send()
        finish(halves, fulls)

    for cp in sends:
        cp.wait()
    keep.wait()


VM = pl.BlockSpec(memory_space=pltpu.VMEM)
DMA = pltpu.SemaphoreType.DMA


def params(cid):
    return pltpu.CompilerParams(collective_id=cid, has_side_effects=True, vmem_limit_bytes=VMEM_LIMIT)


def slices(a):
    return a.T.reshape(2, 4, 2, 2, ROWS, TOK).transpose(3, 0, 2, 1, 4, 5).reshape(8, 448, TOK)


def unslice(a):
    return a.reshape(2, 2, 2, 4, ROWS, TOK).transpose(1, 3, 2, 0, 4, 5).reshape(3584, TOK).T


def local(tokens, cotangent, routes, gates, w_gate, w_up, w_down):
    info = jnp.concatenate([routes.astype(F32), gates, jnp.zeros((TOK, 4), F32)], axis=1).T
    info = jnp.broadcast_to(info[None], (8, 8, TOK))
    packed = jnp.concatenate([slices(tokens), slices(cotangent), info], axis=1)
    w = jnp.concatenate([w_gate, w_up, w_down], axis=0)
    got, wall = pl.pallas_call(
        gather_kernel,
        out_shape=(jax.ShapeDtypeStruct((8, 904, TOK), F32), jax.ShapeDtypeStruct((3, 448, 1024), F32)),
        in_specs=[VM, VM],
        out_specs=(VM, VM),
        scratch_shapes=[DMA((7,)), DMA((7,)), DMA, DMA, DMA((4,)), DMA((4,)), DMA((4, 4)), DMA((4, 4)), DMA((2,))],
        compiler_params=params(0),
    )(packed, w)
    tt, ct = got[:, :448], got[:, 448:896]
    route = got[:, 896:898].astype(jnp.int32)

    def product(a, b):
        return lax.dot_general(a, b, (((1,), (0,)), ((), ())), precision=HIGH)

    pres = [product(tt, wall[0]), product(tt, wall[1]), product(ct, wall[2])]
    chosen = [[(route[:, k] == e)[:, :, None] for e in range(8)] for k in range(2)]
    parts = []
    for k in range(2):
        for p in pres:
            parts.append(sum(jnp.where(chosen[k][e], p[:, :, e * 128 : (e + 1) * 128], 0.0) for e in range(8)))
    partial = jnp.concatenate(parts, axis=2).reshape(2, 4, TOK, 768)
    gate_rows = jnp.repeat(gates, 128, axis=1)
    ga = pl.pallas_call(
        hidden_kernel,
        out_shape=jax.ShapeDtypeStruct((2, 4, TOK, 768), F32),
        in_specs=[VM, VM],
        out_specs=VM,
        scratch_shapes=[
            pltpu.VMEM((4, TOK, 768), F32), pltpu.VMEM((3, TOK, 768), F32),
            DMA((4,)), DMA((4,)), DMA((3,)), DMA((3,)), DMA((3,)), DMA((3,)), DMA((4,)), DMA((4,)),
        ],
        compiler_params=params(1),
    )(partial, gate_rows)
    ga = ga.reshape(8, TOK, 768)

    def dense(i):
        return jnp.concatenate(
            [
                sum(jnp.where(chosen[k][e], ga[:, :, (k * 3 + i) * 128 : (k * 3 + i + 1) * 128], 0.0) for k in range(2))
                for e in range(8)
            ],
            axis=2,
        )

    dgate, dup, dhid = dense(0), dense(1), dense(2)

    def weight(a, g):
        return lax.dot_general(a, g, (((0, 2), (0, 1)), ((), ())), precision=HIGH)

    gw = jnp.stack([weight(tt, dgate), weight(tt, dup), weight(ct, dhid)])

    def back(w, g):
        return lax.dot_general(w, g, (((1,), (2,)), ((), ())), precision=HIGH)

    gt = (back(wall[0], dgate) + back(wall[1], dup)).transpose(1, 0, 2)
    blk = (3, ROWS, 256)
    hlf = (3, ROWS, 128)
    gx, gout = pl.pallas_call(
        scatter_kernel,
        out_shape=(jax.ShapeDtypeStruct((8, 448, TOK), F32), jax.ShapeDtypeStruct(hlf, F32)),
        in_specs=[VM, VM],
        out_specs=(VM, VM),
        scratch_shapes=[
            pltpu.VMEM((4, 2) + blk, F32), pltpu.VMEM((4, 2) + hlf, F32), pltpu.VMEM((4, 2) + blk, F32),
            pltpu.VMEM((2,) + hlf, F32), pltpu.VMEM((2,) + blk, F32), pltpu.VMEM((2,) + blk, F32),
            pltpu.VMEM((2,) + blk, F32), pltpu.VMEM((2,) + hlf, F32), pltpu.VMEM((4,) + blk, F32),
            DMA((7,)), DMA((7,)), DMA, DMA, DMA((4,)), DMA((4,)), DMA((4, 4)), DMA((4, 4)), DMA,
        ],
        compiler_params=params(2),
    )(gt, gw)
    return unslice(gx), gout[0:1], gout[1:2], gout[2:3]


def solution(mesh):
    rows = P(("dp", "expert"), None)
    weights = P("expert", "dp", None)
    return jax.shard_map(
        local,
        mesh=mesh,
        in_specs=(rows, rows, rows, rows, weights, weights, weights),
        out_specs=(rows, weights, weights, weights),
        check_vma=False,
    )
```

```python
import jax
import jax.numpy as jnp
from jax import lax
from jax.experimental import pallas as pl
from jax.experimental.pallas import tpu as pltpu
from jax.sharding import PartitionSpec as P

MESH = pl.DeviceIdType.MESH
VMEM_LIMIT = 62 * 2**20
ROWS = 112
TOK = 128
F32 = jnp.float32
BF16 = jnp.bfloat16
NN = (((1,), (0,)), ((), ()))
NT = (((1,), (1,)), ((), ()))


def coords():
    dp = lax.axis_index("dp")
    e = lax.axis_index("expert")
    return e // 2, (dp // 16) * 2 + e % 2, (dp // 2) % 8, dp % 2


def dev(x, y, z, c):
    x, y, z, c = (x + 4) % 4, (y + 4) % 4, (z + 8) % 8, c % 2
    return ((y // 2) * 8 + z) * 2 + c, x * 2 + y % 2


def remote(src, dst, ss, rs, to):
    return pltpu.make_async_remote_copy(
        src_ref=src, dst_ref=dst, send_sem=ss, recv_sem=rs, device_id=to, device_id_type=MESH
    )


def greet(peers):
    bar = pltpu.get_barrier_semaphore()
    for p in peers:
        pl.semaphore_signal(bar, 1, device_id=p, device_id_type=MESH)
    pl.semaphore_wait(bar, len(peers))


def split(v):
    hi = v.astype(BF16)
    return hi, (v - hi.astype(F32)).astype(BF16)


def dot3(a, b, dims):
    def d(p, q):
        return lax.dot_general(p, q, dims, preferred_element_type=F32)

    return d(a[0], b[0]) + d(a[0], b[1]) + d(a[1], b[0])


PIECES = []
for j in range(28):
    r = j * 128
    found = []
    while r < j * 128 + 128:
        shard = r // ROWS
        stop = min((shard + 1) * ROWS, j * 128 + 128)
        yh, zz, cc = shard // 16, (shard // 2) % 8, shard % 2
        member = (yh * 2 + zz % 2) * 2 + cc
        found.append((member, (zz // 2) * ROWS + r - shard * ROWS, r - j * 128, stop - r))
        r = stop
    PIECES.append(found)

OTHERS = [(dc, dy) for dy in (2, 1, 3, 0) for dc in (0, 1) if (dc, dy) != (0, 0)]


def kernel(
    tok, cot, route, gate, w0, w1, w2, out, gout,
    xs, xg, wg, wsp, tsp, ttsp, infot, part, buf, got, ga, gd, gx, xh, xf, zh, z1, z2, z3,
    s_l, ss_x, rs_x, ss_p, rs_p, ss_z, rs_z, ss_r, rs_r,
    ss_a, rs_a, ss_b, rs_b, ss_c, rs_c, ss_d, rs_d,
    ss_t, rs_t, ss_q, rs_q, ss_y, rs_y, ss_s, rs_s,
):
    x, y, z, c = coords()
    yl = y % 2
    good = (z % 2) == yl
    bad = jnp.logical_not(good)
    me = y * 2 + c
    zi = z // 2
    zp, zm = dev(x, y, z + 1, c), dev(x, y, z - 1, c)
    xp, xm = dev(x + 1, y, z, c), dev(x - 1, y, z, c)
    partner = dev(x, (y // 2) * 2 + 1 - yl, z, c)
    sib = dev(x, y, z, 1 - c)
    greet([dev(x, y + dy, z, c + dc) for dc, dy in OTHERS] + [zp, zm, xp, xm])

    def rows(b):
        return pl.ds(pl.multiple_of(((b + 4) % 4) * ROWS, 16), ROWS)

    def cols(xx):
        return pl.ds(pl.multiple_of(((xx + 4) % 4) * 256, 256), 256)

    def hcols(xx, h):
        return pl.ds(pl.multiple_of(((xx + 4) % 4) * 256 + h * 128, 128), 128)

    def blk(xx, b):
        return wg.at[:, rows(b), cols(xx)]

    def half(xx, b, h):
        return wg.at[:, rows(b), hcols(xx, h)]

    ws = (w0, w1, w2)
    local = [pltpu.make_async_copy(ws[k], wg.at[k, rows(zi), hcols(x, yl)], s_l.at[k]) for k in range(3)]
    shift = [
        remote(ws[k], wg.at[k, rows(zi), hcols(x, yl)], ss_p.at[k], rs_p.at[k], partner) for k in range(3)
    ]

    @pl.when(good)
    def _():
        for cp in local:
            cp.start()

    @pl.when(bad)
    def _():
        for cp in shift:
            cp.start()

    lane = lax.broadcasted_iota(jnp.int32, (TOK, TOK), 1)
    facts = jnp.where(
        lane == 0,
        route[:, 0:1].astype(F32),
        jnp.where(
            lane == 1,
            route[:, 1:2].astype(F32),
            jnp.where(lane == 2, gate[:, 0:1], jnp.where(lane == 3, gate[:, 1:2], 0.0)),
        ),
    )
    facts = facts.T[0:8]
    for m in range(8):
        xs[m, 896:904, :] = facts
    for j in range(28):
        for a, ref in ((0, tok), (1, cot)):
            t = ref[:, j * 128 : (j + 1) * 128].T
            for m, to, frm, n in PIECES[j]:
                xs[m, a * 448 + to : a * 448 + to + n, :] = t[frm : frm + n]
    keep = pltpu.make_async_copy(xs.at[me], xg.at[me], s_l.at[3])
    keep.start()
    tokens_out = []
    for i, (dc, dy) in enumerate(OTHERS):
        y2, c2 = (y + dy) % 4, (c + dc) % 2
        cp = remote(xs.at[y2 * 2 + c2], xg.at[me], ss_x.at[i], rs_x.at[i], dev(x, y2, z, c2))
        cp.start()
        tokens_out.append(cp)

    lo = (z - 1 - yl + 8) // 2
    hi = lo + 1
    b0 = jnp.where(good, zi, lo)
    b1 = jnp.where(good, zi - 1, hi)
    b2 = jnp.where(good, zi + 1, lo - 1)
    b3 = jnp.where(good, zi + 2, hi + 1)

    def zcp(i, ref, to):
        return remote(ref, ref, ss_z.at[i], rs_z.at[i], to)

    def xcp(s, i, ref):
        return remote(ref, ref, ss_r.at[s, i], rs_r.at[s, i], xp if i % 2 == 0 else xm)

    def start_x(s, b):
        xcp(s, 0, blk(x, b)).start()
        xcp(s, 1, blk(x, b)).start()

    def forward_x(s, b):
        xcp(s, 0, blk(x - 1, b)).wait_recv()
        xcp(s, 2, half(x - 1, b, 0)).start()
        xcp(s, 1, blk(x + 1, b)).wait_recv()
        xcp(s, 3, half(x + 1, b, 1)).start()

    def finish_x(s, b):
        xcp(s, 2, half(x - 2, b, 0)).wait_recv()
        xcp(s, 3, half(x + 2, b, 1)).wait_recv()
        for i in range(4):
            (xcp(s, i, blk(x, b)) if i < 2 else xcp(s, i, half(x, b, 0))).wait_send()

    @pl.when(good)
    def _():
        for k in range(3):
            local[k].wait()
            remote(ws[k], wg.at[k, rows(zi), hcols(x, 1 - yl)], ss_p.at[k], rs_p.at[k], partner).wait_recv()
        zcp(0, blk(x, b0), zp).start()
        zcp(2, blk(x, b0), zm).start()
        start_x(0, b0)

    @pl.when(bad)
    def _():
        zcp(0, blk(x, b0), zp).wait_recv()
        zcp(0, blk(x, b0), zp).start()
        start_x(0, b0)
        zcp(2, blk(x, b1), zm).wait_recv()
        zcp(2, blk(x, b1), zm).start()
        start_x(1, b1)

    forward_x(0, b0)

    @pl.when(good)
    def _():
        zcp(0, blk(x, b1), zp).wait_recv()
        zcp(1, blk(x, b1), zp).start()
        start_x(1, b1)
        zcp(2, blk(x, b2), zm).wait_recv()
        zcp(3, blk(x, b2), zm).start()
        start_x(2, b2)

    forward_x(1, b1)

    @pl.when(bad)
    def _():
        zcp(1, blk(x, b2), zp).wait_recv()
        zcp(1, half(x, b2, 0), zp).start()
        start_x(2, b2)
        zcp(3, blk(x, b3), zm).wait_recv()
        zcp(3, half(x, b3, 1), zm).start()
        start_x(3, b3)

    forward_x(2, b2)

    @pl.when(good)
    def _():
        zcp(1, half(x, b3, 0), zp).wait_recv()
        zcp(3, half(x, b3, 1), zm).wait_recv()
        start_x(3, b3)

    forward_x(3, b3)
    for s, b in enumerate((b0, b1, b2, b3)):
        finish_x(s, b)
    zcp(0, blk(x, b0), zp).wait_send()
    zcp(2, blk(x, b0), zm).wait_send()

    @pl.when(good)
    def _():
        zcp(1, blk(x, b1), zp).wait_send()
        zcp(3, blk(x, b1), zm).wait_send()

    @pl.when(bad)
    def _():
        zcp(1, half(x, b1, 0), zp).wait_send()
        zcp(3, half(x, b1, 1), zm).wait_send()
        for cp in shift:
            cp.wait_send()

    def split_w(i, _):
        r = pl.ds(pl.multiple_of(i * 32, 32), 32)
        for k in range(3):
            h, l = split(wg[k, r, :])
            wsp[0, k, r, :] = h
            wsp[1, k, r, :] = l
        return 0

    lax.fori_loop(0, 14, split_w, 0)

    def member_rows(y2, c2):
        return pl.ds(pl.multiple_of(y2 * 256 + c2 * 128, 128), 128)

    def prepare(y2):
        for c2 in range(2):
            m = y2 * 2 + c2
            infot[m, :, 0:8] = xg[m, 896:904, :].T
            for a in range(2):
                v = xg[m, a * 448 : (a + 1) * 448, :]
                h, l = split(v)
                ttsp[0, a, :, member_rows(y2, c2)] = h
                ttsp[1, a, :, member_rows(y2, c2)] = l
                h, l = split(v.T)
                tsp[0, a, c2 * 128 : (c2 + 1) * 128, :] = h
                tsp[1, a, c2 * 128 : (c2 + 1) * 128, :] = l

    def forward(y2):
        r = [
            jnp.concatenate([infot[y2 * 2, :, k : k + 1], infot[y2 * 2 + 1, :, k : k + 1]], axis=0)
            for k in range(2)
        ]
        for kind in range(3):
            a = 1 if kind == 2 else 0
            t = tsp[0, a], tsp[1, a]
            sel = [jnp.zeros((256, 128), F32)] * 2
            for q in range(4):
                cs = slice(q * 256, (q + 1) * 256)
                res = dot3(t, (wsp[0, kind, :, cs], wsp[1, kind, :, cs]), NN)
                for e in range(2):
                    for k in range(2):
                        sel[k] = jnp.where(r[k] == float(q * 2 + e), res[:, e * 128 : (e + 1) * 128], sel[k])
            for k in range(2):
                base = (k * 3 + kind) * 128
                part[y2, 0, :, base : base + 128] = sel[k][0:128]
                part[y2, 1, :, base : base + 128] = sel[k][128:256]

    STEPS = (2, 1, 3, 0)

    def first(i):
        y2 = (y + STEPS[i]) % 4
        return remote(part.at[y2, 1 - c], buf.at[y2], ss_a.at[i], rs_a.at[i], sib)

    def second(i):
        y2 = (y + STEPS[i]) % 4
        return remote(buf.at[y2], got.at[i], ss_b.at[i], rs_b.at[i], dev(x, y2, z, c))

    def merge(i):
        y2 = (y + STEPS[i]) % 4
        first(i).wait_recv()
        buf[y2] = buf[y2] + part[y2, c]
        if i < 3:
            second(i).start()

    keep.wait()
    for i in range(4):
        y2 = (y + STEPS[i]) % 4
        for n, (dc, dy) in enumerate(OTHERS):
            if (4 - dy) % 4 == STEPS[i]:
                tokens_out[n].wait_recv()
        prepare(y2)
        forward(y2)
        first(i).start()
        if i:
            merge(i - 1)
    merge(3)
    total = buf[y]
    for i in range(3):
        second(i).wait_recv()
        total = total + got[i]

    for k in range(2):
        g = gate[:, k : k + 1]
        base = k * 384
        pre_gate = total[:, base : base + 128]
        pre_up = total[:, base + 128 : base + 256]
        back = total[:, base + 256 : base + 384] * g
        s = jax.nn.sigmoid(pre_gate)
        activated = pre_gate * s
        slopes = s * (1.0 + pre_gate * (1.0 - s))
        ga[y, c, :, base : base + 128] = back * pre_up * slopes
        ga[y, c, :, base + 128 : base + 256] = back * activated
        ga[y, c, :, base + 256 : base + 384] = activated * pre_up * g

    def spread(i):
        return remote(ga.at[y, c], ga.at[y, c], ss_c.at[i], rs_c.at[i], dev(x, y + STEPS[i], z, c))

    def pass_on(i, y2):
        return remote(ga.at[y2, c], ga.at[y2, c], ss_d.at[i], rs_d.at[i], sib)

    def expand(y2, c2):
        m = y2 * 2 + c2
        r0, r1 = infot[m, :, 0:1], infot[m, :, 1:2]
        for kind in range(3):
            g0 = ga[y2, c2, :, kind * 128 : (kind + 1) * 128]
            g1 = ga[y2, c2, :, (3 + kind) * 128 : (4 + kind) * 128]
            for e in range(8):
                v = jnp.where(r0 == float(e), g0, jnp.where(r1 == float(e), g1, 0.0))
                h, l = split(v)
                gd[0, kind, member_rows(y2, c2), e * 128 : (e + 1) * 128] = h
                gd[1, kind, member_rows(y2, c2), e * 128 : (e + 1) * 128] = l

    for i in range(3):
        spread(i).start()
    pass_on(3, y).start()
    expand(y, c)
    for i in (1, 2, 0):
        y2 = (y - STEPS[i] + 4) % 4
        remote(ga.at[y2, c], ga.at[y2, c], ss_c.at[i], rs_c.at[i], dev(x, y2, z, c)).wait_recv()
        pass_on(i, y2).start()
        expand(y2, c)
    for i in (3, 1, 2, 0):
        y2 = (y - STEPS[i] + 4) % 4
        remote(ga.at[y2, 1 - c], ga.at[y2, 1 - c], ss_d.at[i], rs_d.at[i], sib).wait_recv()
        expand(y2, 1 - c)
    for i in range(4):
        first(i).wait_send()
        pass_on(i, y).wait_send()
    for i in range(3):
        second(i).wait_send()
        spread(i).wait_send()
    for cp in tokens_out:
        cp.wait_send()

    def weight_grad(xx):
        for kind in range(3):
            a = 1 if kind == 2 else 0
            wg[kind, :, cols(xx)] = dot3(
                (ttsp[0, a], ttsp[1, a]), (gd[0, kind, :, cols(xx)], gd[1, kind, :, cols(xx)]), NN
            )

    o = [jnp.where(good, p, q) for p, q in ((zi + 2, hi + 1), (zi + 1, lo - 1), (zi - 1, hi), (zi, lo))]

    def shalf(s, h):
        return remote(
            half(x + 2, o[s], h), xh.at[s, h], ss_t.at[s, h], rs_t.at[s, h], xp if h == 0 else xm
        )

    def sfull(s, h):
        return remote(
            blk(x + 1 - 2 * h, o[s]), xf.at[s, h], ss_q.at[s, h], rs_q.at[s, h], xp if h == 0 else xm
        )

    weight_grad(x + 2)
    for s in range(4):
        for h in range(2):
            shalf(s, h).start()
    weight_grad(x + 1)
    weight_grad(x - 1)
    for s in range(4):
        for h in range(2):
            shalf(s, h).wait_recv()
            where = (slice(None), rows(o[s]), hcols(x + 1 - 2 * h, h))
            wg[where] = wg[where] + xh[s, h]
            sfull(s, h).start()
    weight_grad(x)

    returns = []
    for i in range(4):
        y2 = (y + STEPS[i]) % 4
        r = pl.ds(pl.multiple_of(y2 * 256, 256), 256)
        res = dot3((wsp[0, 0], wsp[1, 0]), (gd[0, 0, r, :], gd[1, 0, r, :]), NT)
        res = res + dot3((wsp[0, 1], wsp[1, 1]), (gd[0, 1, r, :], gd[1, 1, r, :]), NT)
        xs[y2 * 2, 0:448, :] = res[:, 0:128]
        xs[y2 * 2 + 1, 0:448, :] = res[:, 128:256]
        for n, (dc, dy) in enumerate(OTHERS):
            if dy == STEPS[i]:
                m = y2 * 2 + (c + dc) % 2
                cp = remote(
                    xs.at[m, pl.ds(0, 448), :], gx.at[me], ss_y.at[n], rs_y.at[n], dev(x, y2, z, c + dc)
                )
                cp.start()
                returns.append(cp)
    gx[me] = xs[me, 0:448, :]

    def total_x(s):
        sfull(s, 0).wait_recv()
        sfull(s, 1).wait_recv()
        where = (slice(None), rows(o[s]), cols(x))
        wg[where] = wg[where] + xf[s, 0] + xf[s, 1]

    def add(s, v):
        where = (slice(None), rows(o[s]), cols(x))
        wg[where] = wg[where] + v

    def add_half(s, h, v):
        where = (slice(None), rows(o[s]), hcols(x, h))
        wg[where] = wg[where] + v

    def zs(i, src, dst):
        return remote(src, dst, ss_s.at[i], rs_s.at[i], zp if i < 2 else zm)

    total_x(0)

    @pl.when(good)
    def _():
        zs(0, half(x, o[0], 0), zh.at[0]).start()
        zs(2, half(x, o[0], 1), zh.at[1]).start()

    @pl.when(bad)
    def _():
        zs(0, half(x, o[0], 0), zh.at[0]).wait_recv()
        add_half(0, 0, zh[0])
        zs(0, blk(x, o[0]), z1.at[0]).start()

    total_x(1)

    @pl.when(good)
    def _():
        zs(0, blk(x, o[1]), z1.at[0]).wait_recv()
        add(1, z1[0])
        zs(1, blk(x, o[1]), z2.at[0]).start()

    @pl.when(bad)
    def _():
        zs(2, half(x, o[1], 1), zh.at[1]).wait_recv()
        add_half(1, 1, zh[1])
        zs(2, blk(x, o[1]), z1.at[1]).start()

    total_x(2)

    @pl.when(good)
    def _():
        zs(2, blk(x, o[2]), z1.at[1]).wait_recv()
        add(2, z1[1])
        zs(3, blk(x, o[2]), z2.at[1]).start()

    @pl.when(bad)
    def _():
        zs(1, blk(x, o[2]), z2.at[0]).wait_recv()
        add(2, z2[0])
        zs(1, blk(x, o[2]), z3.at[0]).start()

    total_x(3)

    @pl.when(bad)
    def _():
        zs(3, blk(x, o[3]), z2.at[1]).wait_recv()
        add(3, z2[1])
        zs(3, blk(x, o[3]), z3.at[1]).start()

    for cp in returns:
        cp.wait()
    for j in range(28):
        t = jnp.concatenate([gx[m, to : to + n, :] for m, to, frm, n in PIECES[j]], axis=0)
        out[:, j * 128 : (j + 1) * 128] = t.T

    @pl.when(good)
    def _():
        zs(1, blk(x, o[3]), z3.at[0]).wait_recv()
        zs(3, blk(x, o[3]), z3.at[1]).wait_recv()
        add(3, z3[0] + z3[1])
        back = remote(half(x, o[3], 1 - yl), gout, ss_p.at[0], rs_p.at[3], partner)
        back.start()
        gout[...] = wg[:, rows(o[3]), hcols(x, yl)]
        back.wait_send()
        zs(0, half(x, o[0], 0), zh.at[0]).wait_send()
        zs(2, half(x, o[0], 1), zh.at[1]).wait_send()

    @pl.when(bad)
    def _():
        remote(half(x, o[3], 1 - yl), gout, ss_p.at[0], rs_p.at[3], partner).wait_recv()
        zs(0, blk(x, o[0]), z1.at[0]).wait_send()
        zs(2, blk(x, o[1]), z1.at[1]).wait_send()

    zs(1, blk(x, o[2]), z3.at[0]).wait_send()
    zs(3, blk(x, o[3]), z3.at[1]).wait_send()
    for s in range(4):
        for h in range(2):
            shalf(s, h).wait_send()
            sfull(s, h).wait_send()


def local(tokens, cotangent, routes, gates, w_gate, w_up, w_down):
    vm = pl.BlockSpec(memory_space=pltpu.VMEM)
    dma = pltpu.SemaphoreType.DMA
    full, hlf = (3, ROWS, 256), (3, ROWS, 128)

    def f32(*shape):
        return pltpu.VMEM(shape, F32)

    def bf16(*shape):
        return pltpu.VMEM(shape, BF16)

    out, gout = pl.pallas_call(
        kernel,
        out_shape=(jax.ShapeDtypeStruct((TOK, 3584), F32), jax.ShapeDtypeStruct(hlf, F32)),
        in_specs=[vm] * 7,
        out_specs=(vm, vm),
        scratch_shapes=[
            f32(8, 904, TOK), f32(8, 904, TOK), f32(3, 448, 1024), bf16(2, 3, 448, 1024),
            bf16(2, 2, 256, 448), bf16(2, 2, 448, 1024), f32(8, TOK, 8), f32(4, 2, TOK, 768),
            f32(4, TOK, 768), f32(3, TOK, 768), f32(4, 2, TOK, 768), bf16(2, 3, 1024, 1024),
            f32(8, 448, TOK), f32(4, 2, *hlf), f32(4, 2, *full),
            f32(2, *hlf), f32(2, *full), f32(2, *full), f32(2, *full),
            dma((4,)), dma((7,)), dma((7,)), dma((4,)), dma((4,)), dma((4,)), dma((4,)),
            dma((4, 4)), dma((4, 4)),
            dma((4,)), dma((4,)), dma((3,)), dma((3,)), dma((3,)), dma((3,)), dma((4,)), dma((4,)),
            dma((4, 2)), dma((4, 2)), dma((4, 2)), dma((4, 2)), dma((7,)), dma((7,)), dma((4,)), dma((4,)),
        ],
        compiler_params=pltpu.CompilerParams(
            collective_id=0, has_side_effects=True, vmem_limit_bytes=VMEM_LIMIT
        ),
        cost_estimate=pl.CostEstimate(flops=20_000_000_000, bytes_accessed=8_000_000, transcendentals=40_000),
    )(tokens, cotangent, routes, gates, w_gate[0], w_up[0], w_down[0])
    return out, gout[0:1], gout[1:2], gout[2:3]


def solution(mesh):
    rows = P(("dp", "expert"), None)
    weights = P("expert", "dp", None)
    return jax.shard_map(
        local,
        mesh=mesh,
        in_specs=(rows, rows, rows, rows, weights, weights, weights),
        out_specs=(rows, weights, weights, weights),
        check_vma=False,
    )
```

```python
import jax
import jax.numpy as jnp
from jax import lax
from jax.experimental import pallas as pl
from jax.experimental.pallas import tpu as pltpu
from jax.sharding import PartitionSpec as P

MESH = pl.DeviceIdType.MESH
VMEM_LIMIT = 62 * 2**20
ROWS = 112
TOK = 128
F32 = jnp.float32
BF16 = jnp.bfloat16
NN = (((1,), (0,)), ((), ()))
NT = (((1,), (1,)), ((), ()))


def coords():
    dp = lax.axis_index("dp")
    e = lax.axis_index("expert")
    return e // 2, (dp // 16) * 2 + e % 2, (dp // 2) % 8, dp % 2


def dev(x, y, z, c):
    x, y, z, c = (x + 4) % 4, (y + 4) % 4, (z + 8) % 8, c % 2
    return ((y // 2) * 8 + z) * 2 + c, x * 2 + y % 2


def remote(src, dst, ss, rs, to):
    return pltpu.make_async_remote_copy(
        src_ref=src, dst_ref=dst, send_sem=ss, recv_sem=rs, device_id=to, device_id_type=MESH
    )


def greet(peers):
    bar = pltpu.get_barrier_semaphore()
    for p in peers:
        pl.semaphore_signal(bar, 1, device_id=p, device_id_type=MESH)
    pl.semaphore_wait(bar, len(peers))


def split(v):
    hi = v.astype(BF16)
    return hi, (v - hi.astype(F32)).astype(BF16)


def dot3(a, b, dims):
    def d(p, q):
        return lax.dot_general(p, q, dims, preferred_element_type=F32)

    return d(a[0], b[0]) + d(a[0], b[1]) + d(a[1], b[0])


PIECES = []
for j in range(28):
    r = j * 128
    found = []
    while r < j * 128 + 128:
        shard = r // ROWS
        stop = min((shard + 1) * ROWS, j * 128 + 128)
        yh, zz, cc = shard // 16, (shard // 2) % 8, shard % 2
        member = (yh * 2 + zz % 2) * 2 + cc
        found.append((member, (zz // 2) * ROWS + r - shard * ROWS, r - j * 128, stop - r))
        r = stop
    PIECES.append(found)

OTHERS = [(dc, dy) for dy in (2, 1, 3, 0) for dc in (0, 1) if (dc, dy) != (0, 0)]


def kernel(
    tok, cot, route, gate, w0, w1, w2, out, gout,
    xs, xg, wg, wsp, tsp, ttsp, infot, part, buf, got, ga, gd, gx, xh, xf, zh, z1, z2, z3,
    y0, y1, y2b, y3, yh, yf, ss_bx, rs_bx, ss_bz, rs_bz, rs_by, rs_by2,
    s_l, ss_x, rs_x, ss_p, rs_p, ss_z, rs_z, ss_r, rs_r,
    ss_a, rs_a, ss_b, rs_b, ss_c, rs_c, ss_d, rs_d,
    ss_t, rs_t, ss_q, rs_q, ss_y, rs_y, ss_s, rs_s,
):
    x, y, z, c = coords()
    yl = y % 2
    good = (z % 2) == yl
    bad = jnp.logical_not(good)
    me = y * 2 + c
    zi = z // 2
    zp, zm = dev(x, y, z + 1, c), dev(x, y, z - 1, c)
    xp, xm = dev(x + 1, y, z, c), dev(x - 1, y, z, c)
    partner = dev(x, (y // 2) * 2 + 1 - yl, z, c)
    sib = dev(x, y, z, 1 - c)
    greet([dev(x, y + dy, z, c + dc) for dc, dy in OTHERS] + [zp, zm, xp, xm])

    def rows(b):
        return pl.ds(pl.multiple_of(((b + 4) % 4) * ROWS, 16), ROWS)

    def cols(xx):
        return pl.ds(pl.multiple_of(((xx + 4) % 4) * 256, 256), 256)

    def hcols(xx, h):
        return pl.ds(pl.multiple_of(((xx + 4) % 4) * 256 + h * 128, 128), 128)

    def blk(xx, b):
        return wg.at[0:2, rows(b), cols(xx)]

    def half(xx, b, h):
        return wg.at[0:2, rows(b), hcols(xx, h)]

    def chunk(b, q):
        return wg.at[2, rows(b), pl.ds(q * 512, 512)]

    def bblk(xx):
        return wg.at[2, rows(zi), cols(xx)]

    def bhalf(xx, h):
        return wg.at[2, rows(zi), hcols(xx, h)]

    ws = (w0, w1, w2)
    local = [pltpu.make_async_copy(ws[k], wg.at[k, rows(zi), hcols(x, yl)], s_l.at[k]) for k in range(3)]
    shift = [
        remote(ws[k], wg.at[k, rows(zi), hcols(x, yl)], ss_p.at[k], rs_p.at[k], partner) for k in range(3)
    ]

    @pl.when(good)
    def _():
        for cp in local:
            cp.start()

    @pl.when(bad)
    def _():
        for cp in shift:
            cp.start()

    facts = jnp.concatenate([route[...].astype(F32), gate[...], jnp.zeros((4, TOK), F32)], axis=0)
    for m in range(8):
        xs[m, 896:904, :] = facts
    for j in range(28):
        for a, ref in ((0, tok), (1, cot)):
            t = ref[:, j * 128 : (j + 1) * 128].T
            for m, to, frm, n in PIECES[j]:
                xs[m, a * 448 + to : a * 448 + to + n, :] = t[frm : frm + n]
    keep = pltpu.make_async_copy(xs.at[me], xg.at[me], s_l.at[3])
    keep.start()
    tokens_out = []
    for i, (dc, dy) in enumerate(OTHERS):
        y2, c2 = (y + dy) % 4, (c + dc) % 2
        cp = remote(xs.at[y2 * 2 + c2], xg.at[me], ss_x.at[i], rs_x.at[i], dev(x, y2, z, c2))
        cp.start()
        tokens_out.append(cp)

    lo = (z - 1 - yl + 8) // 2
    hi = lo + 1
    b0 = jnp.where(good, zi, lo)
    b1 = jnp.where(good, zi - 1, hi)
    b2 = jnp.where(good, zi + 1, lo - 1)
    b3 = jnp.where(good, zi + 2, hi + 1)

    def zcp(i, ref, to):
        return remote(ref, ref, ss_z.at[i], rs_z.at[i], to)

    def xcp(s, i, ref):
        return remote(ref, ref, ss_r.at[s, i], rs_r.at[s, i], xp if i % 2 == 0 else xm)

    def start_x(s, b):
        xcp(s, 0, blk(x, b)).start()
        xcp(s, 1, blk(x, b)).start()

    def forward_x(s, b):
        xcp(s, 0, blk(x - 1, b)).wait_recv()
        xcp(s, 2, half(x - 1, b, 0)).start()
        xcp(s, 1, blk(x + 1, b)).wait_recv()
        xcp(s, 3, half(x + 1, b, 1)).start()

    def finish_x(s, b):
        xcp(s, 2, half(x - 2, b, 0)).wait_recv()
        xcp(s, 3, half(x + 2, b, 1)).wait_recv()
        for i in range(4):
            (xcp(s, i, blk(x, b)) if i < 2 else xcp(s, i, half(x, b, 0))).wait_send()

    def bx(i, ref):
        return remote(ref, ref, ss_bx.at[i], rs_bx.at[i], xp if i % 2 == 0 else xm)

    def bz(d, step, q, b):
        return remote(
            chunk(b, q), chunk(b, q), ss_bz.at[d, step, q], rs_bz.at[d, step, q], zm if d else zp
        )

    @pl.when(good)
    def _():
        for k in range(3):
            local[k].wait()
            remote(ws[k], wg.at[k, rows(zi), hcols(x, 1 - yl)], ss_p.at[k], rs_p.at[k], partner).wait_recv()
        zcp(0, blk(x, b0), zp).start()
        zcp(2, blk(x, b0), zm).start()
        bx(0, bblk(x)).start()
        bx(1, bblk(x)).start()
        start_x(0, b0)
        bx(0, bblk(x - 1)).wait_recv()
        bx(2, bhalf(x - 1, 0)).start()
        bx(1, bblk(x + 1)).wait_recv()
        bx(3, bhalf(x + 1, 1)).start()
        bx(2, bhalf(x - 2, 0)).wait_recv()
        bx(3, bhalf(x + 2, 1)).wait_recv()
        for q in (0, 1):
            bz(0, 0, q, b0).start()
            bz(1, 0, 1 - q, b0).start()

    @pl.when(bad)
    def _():
        zcp(0, blk(x, b0), zp).wait_recv()
        zcp(0, blk(x, b0), zp).start()
        start_x(0, b0)
        zcp(2, blk(x, b1), zm).wait_recv()
        zcp(2, blk(x, b1), zm).start()
        start_x(1, b1)

    forward_x(0, b0)

    @pl.when(good)
    def _():
        zcp(0, blk(x, b1), zp).wait_recv()
        zcp(1, blk(x, b1), zp).start()
        start_x(1, b1)
        zcp(2, blk(x, b2), zm).wait_recv()
        zcp(3, blk(x, b2), zm).start()
        start_x(2, b2)

    @pl.when(bad)
    def _():
        for q in (0, 1):
            bz(0, 0, q, b0).wait_recv()
            bz(0, 0, q, b0).start()
            bz(1, 0, 1 - q, b1).wait_recv()
            bz(1, 0, 1 - q, b1).start()

    forward_x(1, b1)

    @pl.when(bad)
    def _():
        zcp(1, blk(x, b2), zp).wait_recv()
        zcp(1, half(x, b2, 0), zp).start()
        start_x(2, b2)
        zcp(3, blk(x, b3), zm).wait_recv()
        zcp(3, half(x, b3, 1), zm).start()
        start_x(3, b3)

    @pl.when(good)
    def _():
        for q in (0, 1):
            bz(0, 0, q, b1).wait_recv()
            bz(0, 1, q, b1).start()
            bz(1, 0, 1 - q, b2).wait_recv()
            bz(1, 1, 1 - q, b2).start()

    forward_x(2, b2)

    @pl.when(good)
    def _():
        zcp(1, half(x, b3, 0), zp).wait_recv()
        zcp(3, half(x, b3, 1), zm).wait_recv()
        start_x(3, b3)

    @pl.when(bad)
    def _():
        bz(0, 1, 0, b2).wait_recv()
        bz(0, 1, 0, b2).start()
        bz(1, 1, 1, b3).wait_recv()
        bz(1, 1, 1, b3).start()
        bz(0, 1, 1, b2).wait_recv()
        bz(1, 1, 0, b3).wait_recv()

    forward_x(3, b3)
    for s, b in enumerate((b0, b1, b2, b3)):
        finish_x(s, b)
    zcp(0, blk(x, b0), zp).wait_send()
    zcp(2, blk(x, b0), zm).wait_send()
    for q in (0, 1):
        bz(0, 0, q, b0).wait_send()
        bz(1, 0, q, b0).wait_send()
    bz(0, 1, 0, b0).wait_send()
    bz(1, 1, 1, b0).wait_send()

    @pl.when(good)
    def _():
        bz(0, 1, 0, b3).wait_recv()
        bz(1, 1, 1, b3).wait_recv()
        zcp(1, blk(x, b1), zp).wait_send()
        zcp(3, blk(x, b1), zm).wait_send()
        bz(0, 1, 1, b1).wait_send()
        bz(1, 1, 0, b1).wait_send()
        for i in range(4):
            bx(i, bblk(x) if i < 2 else bhalf(x, 0)).wait_send()

    @pl.when(bad)
    def _():
        zcp(1, half(x, b1, 0), zp).wait_send()
        zcp(3, half(x, b1, 1), zm).wait_send()
        for cp in shift:
            cp.wait_send()

    def split_w(i, _):
        r = pl.ds(pl.multiple_of(i * 32, 32), 32)
        for k in range(3):
            h, l = split(wg[k, r, :])
            wsp[0, k, r, :] = h
            wsp[1, k, r, :] = l
        return 0

    lax.fori_loop(0, 14, split_w, 0)

    def member_rows(y2, c2):
        return pl.ds(pl.multiple_of(y2 * 256 + c2 * 128, 128), 128)

    def prepare(y2):
        for c2 in range(2):
            m = y2 * 2 + c2
            infot[m, :, 0:8] = xg[m, 896:904, :].T
            for a in range(2):
                v = xg[m, a * 448 : (a + 1) * 448, :]
                h, l = split(v)
                ttsp[0, a, :, member_rows(y2, c2)] = h
                ttsp[1, a, :, member_rows(y2, c2)] = l
                h, l = split(v.T)
                tsp[0, a, c2 * 128 : (c2 + 1) * 128, :] = h
                tsp[1, a, c2 * 128 : (c2 + 1) * 128, :] = l

    def forward(y2):
        r = [
            jnp.concatenate([infot[y2 * 2, :, k : k + 1], infot[y2 * 2 + 1, :, k : k + 1]], axis=0)
            for k in range(2)
        ]
        for kind in range(3):
            a = 1 if kind == 2 else 0
            t = tsp[0, a], tsp[1, a]
            sel = [jnp.zeros((256, 128), F32)] * 2
            for q in range(4):
                cs = slice(q * 256, (q + 1) * 256)
                res = dot3(t, (wsp[0, kind, :, cs], wsp[1, kind, :, cs]), NN)
                for e in range(2):
                    for k in range(2):
                        sel[k] = jnp.where(r[k] == float(q * 2 + e), res[:, e * 128 : (e + 1) * 128], sel[k])
            for k in range(2):
                base = (k * 3 + kind) * 128
                part[y2, 0, :, base : base + 128] = sel[k][0:128]
                part[y2, 1, :, base : base + 128] = sel[k][128:256]

    STEPS = (2, 1, 3, 0)

    def first(i):
        y2 = (y + STEPS[i]) % 4
        return remote(part.at[y2, 1 - c], buf.at[y2], ss_a.at[i], rs_a.at[i], sib)

    def second(i):
        y2 = (y + STEPS[i]) % 4
        return remote(buf.at[y2], got.at[i], ss_b.at[i], rs_b.at[i], dev(x, y2, z, c))

    def merge(i):
        y2 = (y + STEPS[i]) % 4
        first(i).wait_recv()
        buf[y2] = buf[y2] + part[y2, c]
        if i < 3:
            second(i).start()

    keep.wait()
    for i in range(4):
        y2 = (y + STEPS[i]) % 4
        for n, (dc, dy) in enumerate(OTHERS):
            if (4 - dy) % 4 == STEPS[i]:
                tokens_out[n].wait_recv()
        prepare(y2)
        forward(y2)
        first(i).start()
        if i:
            merge(i - 1)
    merge(3)
    total = buf[y]
    for i in range(3):
        second(i).wait_recv()
        total = total + got[i]

    for k in range(2):
        g = infot[me, :, 2 + k : 3 + k]
        base = k * 384
        pre_gate = total[:, base : base + 128]
        pre_up = total[:, base + 128 : base + 256]
        back = total[:, base + 256 : base + 384] * g
        s = jax.nn.sigmoid(pre_gate)
        activated = pre_gate * s
        slopes = s * (1.0 + pre_gate * (1.0 - s))
        ga[y, c, :, base : base + 128] = back * pre_up * slopes
        ga[y, c, :, base + 128 : base + 256] = back * activated
        ga[y, c, :, base + 256 : base + 384] = activated * pre_up * g

    def spread(i):
        return remote(ga.at[y, c], ga.at[y, c], ss_c.at[i], rs_c.at[i], dev(x, y + STEPS[i], z, c))

    def pass_on(i, y2):
        return remote(ga.at[y2, c], ga.at[y2, c], ss_d.at[i], rs_d.at[i], sib)

    def expand(y2, c2):
        m = y2 * 2 + c2
        r0, r1 = infot[m, :, 0:1], infot[m, :, 1:2]
        for kind in range(3):
            g0 = ga[y2, c2, :, kind * 128 : (kind + 1) * 128]
            g1 = ga[y2, c2, :, (3 + kind) * 128 : (4 + kind) * 128]
            for e in range(8):
                v = jnp.where(r0 == float(e), g0, jnp.where(r1 == float(e), g1, 0.0))
                h, l = split(v)
                gd[0, kind, member_rows(y2, c2), e * 128 : (e + 1) * 128] = h
                gd[1, kind, member_rows(y2, c2), e * 128 : (e + 1) * 128] = l

    for i in range(3):
        spread(i).start()
    pass_on(3, y).start()
    expand(y, c)
    for i in (1, 2, 0):
        y2 = (y - STEPS[i] + 4) % 4
        remote(ga.at[y2, c], ga.at[y2, c], ss_c.at[i], rs_c.at[i], dev(x, y2, z, c)).wait_recv()
        pass_on(i, y2).start()
        expand(y2, c)
    for i in (3, 1, 2, 0):
        y2 = (y - STEPS[i] + 4) % 4
        remote(ga.at[y2, 1 - c], ga.at[y2, 1 - c], ss_d.at[i], rs_d.at[i], sib).wait_recv()
        expand(y2, 1 - c)
    for i in range(4):
        first(i).wait_send()
        pass_on(i, y).wait_send()
    for i in range(3):
        second(i).wait_send()
        spread(i).wait_send()
    for cp in tokens_out:
        cp.wait_send()

    def weight_grad(xx):
        for kind in range(2):
            wg[kind, :, cols(xx)] = dot3(
                (ttsp[0, 0], ttsp[1, 0]), (gd[0, kind, :, cols(xx)], gd[1, kind, :, cols(xx)]), NN
            )

    def weight_grad_b(q):
        cs = slice(q * 512, q * 512 + 512)
        wg[2, :, cs] = dot3((ttsp[0, 1], ttsp[1, 1]), (gd[0, 2, :, cs], gd[1, 2, :, cs]), NN)

    o = [jnp.where(good, p, q) for p, q in ((zi + 2, hi + 1), (zi + 1, lo - 1), (zi - 1, hi), (zi, lo))]

    def shalf(s, h):
        return remote(
            half(x + 2, o[s], h), xh.at[s, h], ss_t.at[s, h], rs_t.at[s, h], xp if h == 0 else xm
        )

    def sfull(s, h):
        return remote(
            blk(x + 1 - 2 * h, o[s]), xf.at[s, h], ss_q.at[s, h], rs_q.at[s, h], xp if h == 0 else xm
        )

    def by(d, step, q, b, dst):
        return remote(
            chunk(b, q), dst.at[d, :, pl.ds(q * 512, 512)],
            ss_bz.at[d, step, q], rs_by.at[d, step, q], zm if d else zp,
        )

    def take(d, step, q, b, dst):
        by(d, step, q, b, dst).wait_recv()
        where = (2, rows(b), slice(q * 512, q * 512 + 512))
        wg[where] = wg[where] + dst[d, :, q * 512 : q * 512 + 512]

    weight_grad(x + 2)
    for s in range(4):
        for h in range(2):
            shalf(s, h).start()
    weight_grad_b(0)

    @pl.when(good)
    def _():
        by(0, 0, 0, zi + 2, y0).start()

    @pl.when(bad)
    def _():
        by(1, 0, 0, lo - 1, y1).start()

    weight_grad_b(1)

    @pl.when(good)
    def _():
        by(1, 0, 1, zi + 2, y0).start()

    @pl.when(bad)
    def _():
        by(0, 0, 1, hi + 1, y1).start()

    weight_grad(x + 1)
    weight_grad(x - 1)

    @pl.when(bad)
    def _():
        take(0, 0, 0, hi + 1, y0)
        by(0, 0, 0, hi + 1, y1).start()
        take(1, 0, 1, lo - 1, y0)
        by(1, 0, 1, lo - 1, y1).start()

    for s in range(4):
        for h in range(2):
            shalf(s, h).wait_recv()
            where = (slice(0, 2), rows(o[s]), hcols(x + 1 - 2 * h, h))
            wg[where] = wg[where] + xh[s, h]
            sfull(s, h).start()

    @pl.when(good)
    def _():
        take(0, 0, 1, zi + 1, y1)
        by(0, 1, 1, zi + 1, y2b).start()
        take(1, 0, 0, zi - 1, y1)
        by(1, 1, 0, zi - 1, y2b).start()

    weight_grad(x)

    @pl.when(good)
    def _():
        take(0, 0, 0, zi + 1, y1)
        by(0, 1, 0, zi + 1, y2b).start()
        take(1, 0, 1, zi - 1, y1)
        by(1, 1, 1, zi - 1, y2b).start()

    returns = []

    def token_grad(i):
        y2 = (y + STEPS[i]) % 4
        r = pl.ds(pl.multiple_of(y2 * 256, 256), 256)
        res = dot3((wsp[0, 0], wsp[1, 0]), (gd[0, 0, r, :], gd[1, 0, r, :]), NT)
        res = res + dot3((wsp[0, 1], wsp[1, 1]), (gd[0, 1, r, :], gd[1, 1, r, :]), NT)
        xs[y2 * 2, 0:448, :] = res[:, 0:128]
        xs[y2 * 2 + 1, 0:448, :] = res[:, 128:256]
        for n, (dc, dy) in enumerate(OTHERS):
            if dy == STEPS[i]:
                m = y2 * 2 + (c + dc) % 2
                cp = remote(
                    xs.at[m, pl.ds(0, 448), :], gx.at[me], ss_y.at[n], rs_y.at[n], dev(x, y2, z, c + dc)
                )
                cp.start()
                returns.append(cp)

    token_grad(0)
    token_grad(1)

    @pl.when(bad)
    def _():
        take(0, 1, 1, hi, y2b)
        by(0, 1, 1, hi, y3).start()
        take(1, 1, 0, lo, y2b)
        by(1, 1, 0, lo, y3).start()

    token_grad(2)

    @pl.when(bad)
    def _():
        take(0, 1, 0, hi, y2b)
        by(0, 1, 0, hi, y3).start()
        take(1, 1, 1, lo, y2b)
        by(1, 1, 1, lo, y3).start()

    token_grad(3)
    gx[me] = xs[me, 0:448, :]

    def total_x(s):
        sfull(s, 0).wait_recv()
        sfull(s, 1).wait_recv()
        where = (slice(0, 2), rows(o[s]), cols(x))
        wg[where] = wg[where] + xf[s, 0] + xf[s, 1]

    def add(s, v):
        where = (slice(0, 2), rows(o[s]), cols(x))
        wg[where] = wg[where] + v

    def add_half(s, h, v):
        where = (slice(0, 2), rows(o[s]), hcols(x, h))
        wg[where] = wg[where] + v

    def zs(i, src, dst):
        return remote(src, dst, ss_s.at[i], rs_s.at[i], zp if i < 2 else zm)

    total_x(0)

    @pl.when(good)
    def _():
        zs(0, half(x, o[0], 0), zh.at[0]).start()
        zs(2, half(x, o[0], 1), zh.at[1]).start()

    @pl.when(bad)
    def _():
        zs(0, half(x, o[0], 0), zh.at[0]).wait_recv()
        add_half(0, 0, zh[0])
        zs(0, blk(x, o[0]), z1.at[0]).start()

    total_x(1)

    @pl.when(good)
    def _():
        zs(0, blk(x, o[1]), z1.at[0]).wait_recv()
        add(1, z1[0])
        zs(1, blk(x, o[1]), z2.at[0]).start()

    @pl.when(bad)
    def _():
        zs(2, half(x, o[1], 1), zh.at[1]).wait_recv()
        add_half(1, 1, zh[1])
        zs(2, blk(x, o[1]), z1.at[1]).start()

    def bh(h):
        return remote(bhalf(x + 2, h), yh.at[h], ss_bx.at[h], rs_by2.at[h], xm if h else xp)

    def bf(h):
        return remote(bblk(x + 1 - 2 * h), yf.at[h], ss_bx.at[2 + h], rs_by2.at[2 + h], xm if h else xp)

    @pl.when(good)
    def _():
        for q in (0, 1):
            take(0, 1, 1 - q, zi, y3)
            take(1, 1, q, zi, y3)
        bh(0).start()
        bh(1).start()

    total_x(2)

    @pl.when(good)
    def _():
        for h in range(2):
            bh(h).wait_recv()
            where = (2, rows(zi), hcols(x + 1 - 2 * h, h))
            wg[where] = wg[where] + yh[h]
            bf(h).start()
        zs(2, blk(x, o[2]), z1.at[1]).wait_recv()
        add(2, z1[1])
        zs(3, blk(x, o[2]), z2.at[1]).start()

    @pl.when(bad)
    def _():
        zs(1, blk(x, o[2]), z2.at[0]).wait_recv()
        add(2, z2[0])
        zs(1, blk(x, o[2]), z3.at[0]).start()

    total_x(3)

    @pl.when(bad)
    def _():
        zs(3, blk(x, o[3]), z2.at[1]).wait_recv()
        add(3, z2[1])
        zs(3, blk(x, o[3]), z3.at[1]).start()

    for cp in returns:
        cp.wait()
    for j in range(28):
        t = jnp.concatenate([gx[m, to : to + n, :] for m, to, frm, n in PIECES[j]], axis=0)
        out[:, j * 128 : (j + 1) * 128] = t.T

    @pl.when(good)
    def _():
        zs(1, blk(x, o[3]), z3.at[0]).wait_recv()
        zs(3, blk(x, o[3]), z3.at[1]).wait_recv()
        add(3, z3[0] + z3[1])
        bf(0).wait_recv()
        bf(1).wait_recv()
        where = (2, rows(zi), cols(x))
        wg[where] = wg[where] + yf[0] + yf[1]
        back = remote(wg.at[:, rows(zi), hcols(x, 1 - yl)], gout, ss_p.at[0], rs_p.at[3], partner)
        back.start()
        gout[...] = wg[:, rows(zi), hcols(x, yl)]
        back.wait_send()
        zs(0, half(x, o[0], 0), zh.at[0]).wait_send()
        zs(2, half(x, o[0], 1), zh.at[1]).wait_send()
        by(0, 0, 0, zi + 2, y0).wait_send()
        by(1, 0, 1, zi + 2, y0).wait_send()
        for h in range(2):
            bh(h).wait_send()
            bf(h).wait_send()

    @pl.when(bad)
    def _():
        remote(wg.at[:, rows(zi), hcols(x, 1 - yl)], gout, ss_p.at[0], rs_p.at[3], partner).wait_recv()
        zs(0, blk(x, o[0]), z1.at[0]).wait_send()
        zs(2, blk(x, o[1]), z1.at[1]).wait_send()
        for q in (0, 1):
            by(0, 0, q, hi + 1, y1).wait_send()
            by(1, 0, q, lo - 1, y1).wait_send()

    for q in (0, 1):
        by(0, 1, q, zi, y2b).wait_send()
        by(1, 1, q, zi, y2b).wait_send()
    zs(1, blk(x, o[2]), z3.at[0]).wait_send()
    zs(3, blk(x, o[3]), z3.at[1]).wait_send()
    for s in range(4):
        for h in range(2):
            shalf(s, h).wait_send()
            sfull(s, h).wait_send()


def local(tokens, cotangent, routes, gates, w_gate, w_up, w_down):
    vm = pl.BlockSpec(memory_space=pltpu.VMEM)
    dma = pltpu.SemaphoreType.DMA
    full, hlf = (2, ROWS, 256), (2, ROWS, 128)

    def f32(*shape):
        return pltpu.VMEM(shape, F32)

    def bf16(*shape):
        return pltpu.VMEM(shape, BF16)

    out, gout = pl.pallas_call(
        kernel,
        out_shape=(jax.ShapeDtypeStruct((TOK, 3584), F32), jax.ShapeDtypeStruct((3, ROWS, 128), F32)),
        in_specs=[vm] * 7,
        out_specs=(vm, vm),
        scratch_shapes=[
            f32(8, 904, TOK), f32(8, 904, TOK), f32(3, 448, 1024), bf16(2, 3, 448, 1024),
            bf16(2, 2, 256, 448), bf16(2, 2, 448, 1024), f32(8, TOK, 8), f32(4, 2, TOK, 768),
            f32(4, TOK, 768), f32(3, TOK, 768), f32(4, 2, TOK, 768), bf16(2, 3, 1024, 1024),
            f32(8, 448, TOK), f32(4, 2, *hlf), f32(4, 2, *full),
            f32(2, *hlf), f32(2, *full), f32(2, *full), f32(2, *full),
            f32(2, ROWS, 1024), f32(2, ROWS, 1024), f32(2, ROWS, 1024), f32(2, ROWS, 1024),
            f32(2, ROWS, 128), f32(2, ROWS, 256),
            dma((4,)), dma((4,)), dma((2, 2, 2)), dma((2, 2, 2)), dma((2, 2, 2)), dma((4,)),
            dma((4,)), dma((7,)), dma((7,)), dma((4,)), dma((4,)), dma((4,)), dma((4,)),
            dma((4, 4)), dma((4, 4)),
            dma((4,)), dma((4,)), dma((3,)), dma((3,)), dma((3,)), dma((3,)), dma((4,)), dma((4,)),
            dma((4, 2)), dma((4, 2)), dma((4, 2)), dma((4, 2)), dma((7,)), dma((7,)), dma((4,)), dma((4,)),
        ],
        compiler_params=pltpu.CompilerParams(
            collective_id=0, has_side_effects=True, vmem_limit_bytes=VMEM_LIMIT
        ),
        cost_estimate=pl.CostEstimate(flops=20_000_000_000, bytes_accessed=8_000_000, transcendentals=40_000),
    )(tokens, cotangent, routes.T, gates.T, w_gate[0], w_up[0], w_down[0])
    return out, gout[0:1], gout[1:2], gout[2:3]


def solution(mesh):
    rows = P(("dp", "expert"), None)
    weights = P("expert", "dp", None)
    return jax.shard_map(
        local,
        mesh=mesh,
        in_specs=(rows, rows, rows, rows, weights, weights, weights),
        out_specs=(rows, weights, weights, weights),
        check_vma=False,
    )
```

```python
import jax
import jax.numpy as jnp
from jax import lax
from jax.experimental import pallas as pl
from jax.experimental.pallas import tpu as pltpu
from jax.sharding import PartitionSpec as P

MESH = pl.DeviceIdType.MESH
VMEM_LIMIT = 62 * 2**20
ROWS = 112
TOK = 128
F32 = jnp.float32
BF16 = jnp.bfloat16
NN = (((1,), (0,)), ((), ()))
NT = (((1,), (1,)), ((), ()))


def coords():
    dp = lax.axis_index("dp")
    e = lax.axis_index("expert")
    return e // 2, (dp // 16) * 2 + e % 2, (dp // 2) % 8, dp % 2


def dev(x, y, z, c):
    x, y, z, c = (x + 4) % 4, (y + 4) % 4, (z + 8) % 8, c % 2
    return ((y // 2) * 8 + z) * 2 + c, x * 2 + y % 2


def remote(src, dst, ss, rs, to):
    return pltpu.make_async_remote_copy(
        src_ref=src, dst_ref=dst, send_sem=ss, recv_sem=rs, device_id=to, device_id_type=MESH
    )


def greet(peers):
    bar = pltpu.get_barrier_semaphore()
    for p in peers:
        pl.semaphore_signal(bar, 1, device_id=p, device_id_type=MESH)
    pl.semaphore_wait(bar, len(peers))


def split(v):
    hi = v.astype(BF16)
    return hi, (v - hi.astype(F32)).astype(BF16)


def dot3(a, b, dims):
    def d(p, q):
        return lax.dot_general(p, q, dims, preferred_element_type=F32)

    return d(a[0], b[0]) + d(a[0], b[1]) + d(a[1], b[0])


PIECES = []
for j in range(28):
    r = j * 128
    found = []
    while r < j * 128 + 128:
        shard = r // ROWS
        stop = min((shard + 1) * ROWS, j * 128 + 128)
        yh, zz, cc = shard // 16, (shard // 2) % 8, shard % 2
        member = (yh * 2 + zz % 2) * 2 + cc
        found.append((member, (zz // 2) * ROWS + r - shard * ROWS, r - j * 128, stop - r))
        r = stop
    PIECES.append(found)

OTHERS = [(dc, dy) for dy in (2, 1, 3, 0) for dc in (0, 1) if (dc, dy) != (0, 0)]


def kernel(
    tok, cot, route, gate, w0, w1, w2, out, gout,
    xs, xc, xg, cg, wg, wsp, tsp, csp, ttsp, infot, part, buf, got_h, got, ga, gd, xh, xf, zh, z1, z2, z3,
    y0, y1, y2b, y3, yh, yf, ss_bx, rs_bx, ss_bz, rs_bz, rs_by, rs_by2,
    s_l, ss_x, rs_x, ss_xc, rs_xc, ss_p, rs_p, ss_z, rs_z, ss_r, rs_r,
    ss_a, rs_a, ss_b, rs_b, ss_c, rs_c, ss_d, rs_d,
    ss_t, rs_t, ss_q, rs_q, ss_y, rs_y, ss_s, rs_s,
):
    x, y, z, c = coords()
    yl = y % 2
    good = (z % 2) == yl
    bad = jnp.logical_not(good)
    me = y * 2 + c
    zi = z // 2
    zp, zm = dev(x, y, z + 1, c), dev(x, y, z - 1, c)
    xp, xm = dev(x + 1, y, z, c), dev(x - 1, y, z, c)
    partner = dev(x, (y // 2) * 2 + 1 - yl, z, c)
    sib = dev(x, y, z, 1 - c)
    greet([dev(x, y + dy, z, c + dc) for dc, dy in OTHERS] + [zp, zm, xp, xm])

    def rows(b):
        return pl.ds(pl.multiple_of(((b + 4) % 4) * ROWS, 16), ROWS)

    def cols(xx):
        return pl.ds(pl.multiple_of(((xx + 4) % 4) * 256, 256), 256)

    def hcols(xx, h):
        return pl.ds(pl.multiple_of(((xx + 4) % 4) * 256 + h * 128, 128), 128)

    def blk(xx, b):
        return wg.at[0:2, rows(b), cols(xx)]

    def half(xx, b, h):
        return wg.at[0:2, rows(b), hcols(xx, h)]

    def chunk(b, q):
        return wg.at[2, rows(b), pl.ds(q * 512, 512)]

    def bblk(xx):
        return wg.at[2, rows(zi), cols(xx)]

    def bhalf(xx, h):
        return wg.at[2, rows(zi), hcols(xx, h)]

    ws = (w0, w1, w2)
    local = [pltpu.make_async_copy(ws[k], wg.at[k, rows(zi), hcols(x, yl)], s_l.at[k]) for k in range(3)]
    shift = [
        remote(ws[k], wg.at[k, rows(zi), hcols(x, yl)], ss_p.at[k], rs_p.at[k], partner) for k in range(3)
    ]

    @pl.when(good)
    def _():
        for cp in local:
            cp.start()

    @pl.when(bad)
    def _():
        for cp in shift:
            cp.start()

    facts = jnp.concatenate([route[...].astype(F32), gate[...], jnp.zeros((4, TOK), F32)], axis=0)
    for m in range(8):
        xs[m, 448:456, :] = facts

    def transpose(ref, dst):
        for j in range(28):
            t = ref[:, j * 128 : (j + 1) * 128].T
            for m, to, frm, n in PIECES[j]:
                dst[m, to : to + n, :] = t[frm : frm + n]

    def group(src, dst, ss, rs):
        cps = []
        for i, (dc, dy) in enumerate(OTHERS):
            y2, c2 = (y + dy) % 4, (c + dc) % 2
            cps.append(remote(src.at[y2 * 2 + c2], dst.at[me], ss.at[i], rs.at[i], dev(x, y2, z, c2)))
        return cps

    transpose(tok, xs)
    keep = pltpu.make_async_copy(xs.at[me], xg.at[me], s_l.at[3])
    keep.start()
    tokens_out = group(xs, xg, ss_x, rs_x)
    for cp in tokens_out:
        cp.start()
    transpose(cot, xc)
    keep_c = pltpu.make_async_copy(xc.at[me], cg.at[me], s_l.at[4])
    keep_c.start()
    cot_out = group(xc, cg, ss_xc, rs_xc)

    def member_rows(y2, c2):
        return pl.ds(pl.multiple_of(y2 * 256 + c2 * 128, 128), 128)

    def prepare_t(y2):
        for c2 in range(2):
            m = y2 * 2 + c2
            infot[m, :, 0:8] = xg[m, 448:456, :].T
            v = xg[m, 0:448, :]
            r = member_rows(y2, c2)
            ttsp[0, 0, :, r], ttsp[1, 0, :, r] = split(v)
            tsp[0, r, :], tsp[1, r, :] = split(v.T)

    def prepare_c(y2):
        for c2 in range(2):
            v = cg[y2 * 2 + c2]
            r = member_rows(y2, c2)
            ttsp[0, 1, :, r], ttsp[1, 1, :, r] = split(v)
            csp[0, c2 * 128 : (c2 + 1) * 128, :], csp[1, c2 * 128 : (c2 + 1) * 128, :] = split(v.T)

    lo = (z - 1 - yl + 8) // 2
    hi = lo + 1
    b0 = jnp.where(good, zi, lo)
    b1 = jnp.where(good, zi - 1, hi)
    b2 = jnp.where(good, zi + 1, lo - 1)
    b3 = jnp.where(good, zi + 2, hi + 1)

    def zcp(i, ref, to):
        return remote(ref, ref, ss_z.at[i], rs_z.at[i], to)

    def xcp(s, i, ref):
        return remote(ref, ref, ss_r.at[s, i], rs_r.at[s, i], xp if i % 2 == 0 else xm)

    def start_x(s, b):
        xcp(s, 0, blk(x, b)).start()
        xcp(s, 1, blk(x, b)).start()

    def forward_x(s, b):
        xcp(s, 0, blk(x - 1, b)).wait_recv()
        xcp(s, 2, half(x - 1, b, 0)).start()
        xcp(s, 1, blk(x + 1, b)).wait_recv()
        xcp(s, 3, half(x + 1, b, 1)).start()

    def finish_x(s, b):
        xcp(s, 2, half(x - 2, b, 0)).wait_recv()
        xcp(s, 3, half(x + 2, b, 1)).wait_recv()
        for i in range(4):
            (xcp(s, i, blk(x, b)) if i < 2 else xcp(s, i, half(x, b, 0))).wait_send()

    def bx(i, ref):
        return remote(ref, ref, ss_bx.at[i], rs_bx.at[i], xp if i % 2 == 0 else xm)

    def bz(d, step, q, b):
        return remote(
            chunk(b, q), chunk(b, q), ss_bz.at[d, step, q], rs_bz.at[d, step, q], zm if d else zp
        )

    @pl.when(good)
    def _():
        for k in range(3):
            local[k].wait()
            remote(ws[k], wg.at[k, rows(zi), hcols(x, 1 - yl)], ss_p.at[k], rs_p.at[k], partner).wait_recv()
        zcp(0, blk(x, b0), zp).start()
        zcp(2, blk(x, b0), zm).start()
        bx(0, bblk(x)).start()
        bx(1, bblk(x)).start()
        start_x(0, b0)
        bx(0, bblk(x - 1)).wait_recv()
        bx(2, bhalf(x - 1, 0)).start()
        bx(1, bblk(x + 1)).wait_recv()
        bx(3, bhalf(x + 1, 1)).start()
        bx(2, bhalf(x - 2, 0)).wait_recv()
        bx(3, bhalf(x + 2, 1)).wait_recv()
        for q in (0, 1):
            bz(0, 0, q, b0).start()
            bz(1, 0, 1 - q, b0).start()

    @pl.when(bad)
    def _():
        zcp(0, blk(x, b0), zp).wait_recv()
        zcp(0, blk(x, b0), zp).start()
        start_x(0, b0)
        zcp(2, blk(x, b1), zm).wait_recv()
        zcp(2, blk(x, b1), zm).start()
        start_x(1, b1)

    forward_x(0, b0)

    @pl.when(good)
    def _():
        zcp(0, blk(x, b1), zp).wait_recv()
        zcp(1, blk(x, b1), zp).start()
        start_x(1, b1)
        zcp(2, blk(x, b2), zm).wait_recv()
        zcp(3, blk(x, b2), zm).start()
        start_x(2, b2)

    @pl.when(bad)
    def _():
        for q in (0, 1):
            bz(0, 0, q, b0).wait_recv()
            bz(0, 0, q, b0).start()
            bz(1, 0, 1 - q, b1).wait_recv()
            bz(1, 0, 1 - q, b1).start()

    forward_x(1, b1)

    @pl.when(bad)
    def _():
        zcp(1, blk(x, b2), zp).wait_recv()
        zcp(1, half(x, b2, 0), zp).start()
        start_x(2, b2)
        zcp(3, blk(x, b3), zm).wait_recv()
        zcp(3, half(x, b3, 1), zm).start()
        start_x(3, b3)

    @pl.when(good)
    def _():
        for q in (0, 1):
            bz(0, 0, q, b1).wait_recv()
            bz(0, 1, q, b1).start()
            bz(1, 0, 1 - q, b2).wait_recv()
            bz(1, 1, 1 - q, b2).start()

    for cp in tokens_out:
        cp.wait_send()
    for cp in cot_out:
        cp.start()
    forward_x(2, b2)

    @pl.when(good)
    def _():
        zcp(1, half(x, b3, 0), zp).wait_recv()
        zcp(3, half(x, b3, 1), zm).wait_recv()
        start_x(3, b3)

    @pl.when(bad)
    def _():
        bz(0, 1, 0, b2).wait_recv()
        bz(0, 1, 0, b2).start()
        bz(1, 1, 1, b3).wait_recv()
        bz(1, 1, 1, b3).start()
        bz(0, 1, 1, b2).wait_recv()
        bz(1, 1, 0, b3).wait_recv()

    keep.wait()
    for cp in tokens_out:
        cp.wait_recv()
    for i in range(4):
        prepare_t((y + i) % 4)
    forward_x(3, b3)
    for s, b in enumerate((b0, b1, b2, b3)):
        finish_x(s, b)
    zcp(0, blk(x, b0), zp).wait_send()
    zcp(2, blk(x, b0), zm).wait_send()
    for q in (0, 1):
        bz(0, 0, q, b0).wait_send()
        bz(1, 0, q, b0).wait_send()
    bz(0, 1, 0, b0).wait_send()
    bz(1, 1, 1, b0).wait_send()

    @pl.when(good)
    def _():
        bz(0, 1, 0, b3).wait_recv()
        bz(1, 1, 1, b3).wait_recv()
        zcp(1, blk(x, b1), zp).wait_send()
        zcp(3, blk(x, b1), zm).wait_send()
        bz(0, 1, 1, b1).wait_send()
        bz(1, 1, 0, b1).wait_send()
        for i in range(4):
            bx(i, bblk(x) if i < 2 else bhalf(x, 0)).wait_send()

    @pl.when(bad)
    def _():
        zcp(1, half(x, b1, 0), zp).wait_send()
        zcp(3, half(x, b1, 1), zm).wait_send()
        for cp in shift:
            cp.wait_send()

    def split_w(kinds):
        def step(i, _):
            r = pl.ds(pl.multiple_of(i * 32, 32), 32)
            for k in kinds:
                h, l = split(wg[k, r, :])
                wsp[0, k, r, :] = h
                wsp[1, k, r, :] = l
            return 0

        lax.fori_loop(0, 14, step, 0)

    def forward(y2, kinds):
        r = [
            jnp.concatenate([infot[y2 * 2, :, k : k + 1], infot[y2 * 2 + 1, :, k : k + 1]], axis=0)
            for k in range(2)
        ]
        rr = pl.ds(pl.multiple_of(y2 * 256, 256), 256)
        for kind in kinds:
            t = (csp[0], csp[1]) if kind == 2 else (tsp[0, rr, :], tsp[1, rr, :])
            sel = [jnp.zeros((256, 128), F32)] * 2
            for q in range(4):
                cs = slice(q * 256, (q + 1) * 256)
                res = dot3(t, (wsp[0, kind, :, cs], wsp[1, kind, :, cs]), NN)
                for e in range(2):
                    for k in range(2):
                        sel[k] = jnp.where(r[k] == float(q * 2 + e), res[:, e * 128 : (e + 1) * 128], sel[k])
            for k in range(2):
                base = (kind * 2 + k) * 128
                part[y2, 0, :, base : base + 128] = sel[k][0:128]
                part[y2, 1, :, base : base + 128] = sel[k][128:256]

    STEPS = (2, 1, 3, 0)
    COLS = (pl.ds(0, 512), pl.ds(512, 256))

    def first(p, i):
        y2 = (y + STEPS[i]) % 4
        return remote(
            part.at[y2, 1 - c, :, COLS[p]], buf.at[y2, :, COLS[p]], ss_a.at[p, i], rs_a.at[p, i], sib
        )

    yp, ym = dev(x, y + 1, z, c), dev(x, y - 1, z, c)

    def ring_half(p, h):
        return remote(
            buf.at[(y + 2) % 4, pl.ds(64 * h, 64), COLS[p]], got_h.at[h, :, COLS[p]],
            ss_b.at[p, h], rs_b.at[p, h], ym if h else yp,
        )

    def ring_full(p, h):
        return remote(
            buf.at[(y + 1 + 2 * h) % 4, :, COLS[p]], got.at[h, :, COLS[p]],
            ss_b.at[p, 2 + h], rs_b.at[p, 2 + h], ym if h else yp,
        )

    def merge(p, i):
        y2 = (y + STEPS[i]) % 4
        first(p, i).wait_recv()
        buf[y2, :, COLS[p]] = buf[y2, :, COLS[p]] + part[y2, c, :, COLS[p]]
        if i == 0:
            ring_half(p, 0).start()
            ring_half(p, 1).start()
        elif i < 3:
            h = i - 1
            ring_half(p, h).wait_recv()
            r = pl.ds(64 * h, 64)
            buf[y2, r, COLS[p]] = buf[y2, r, COLS[p]] + got_h[h, :, COLS[p]]
            ring_full(p, h).start()

    split_w((0, 1))
    for i in range(4):
        forward((y + STEPS[i]) % 4, (0, 1))
        first(0, i).start()
        if i == 1:
            merge(0, 0)
    split_w((2,))
    merge(0, 1)
    keep_c.wait()
    for i in range(4):
        y2 = (y + STEPS[i]) % 4
        for n, (dc, dy) in enumerate(OTHERS):
            if (4 - dy) % 4 == STEPS[i]:
                cot_out[n].wait_recv()
        prepare_c(y2)
        forward(y2, (2,))
        first(1, i).start()
        if i == 0:
            merge(0, 2)
            merge(0, 3)
        else:
            merge(1, i - 1)
    merge(1, 3)
    for p in range(2):
        for h in range(2):
            ring_full(p, h).wait_recv()
    total = buf[y] + got[0] + got[1]

    for k in range(2):
        g = infot[me, :, 2 + k : 3 + k]
        base = k * 384
        pre_gate = total[:, k * 128 : k * 128 + 128]
        pre_up = total[:, k * 128 + 256 : k * 128 + 384]
        back = total[:, k * 128 + 512 : k * 128 + 640] * g
        s = jax.nn.sigmoid(pre_gate)
        activated = pre_gate * s
        slopes = s * (1.0 + pre_gate * (1.0 - s))
        ga[y, c, :, base : base + 128] = back * pre_up * slopes
        ga[y, c, :, base + 128 : base + 256] = back * activated
        ga[y, c, :, base + 256 : base + 384] = activated * pre_up * g

    def spread(h):
        return remote(ga.at[y, c], ga.at[y, c], ss_c.at[h], rs_c.at[h], ym if h else yp)

    def spread_half(h, y2):
        ref = ga.at[y2 % 4, c, pl.ds(64 * h, 64), :]
        return remote(ref, ref, ss_c.at[2 + h], rs_c.at[2 + h], ym if h else yp)

    def pass_on(i, y2):
        return remote(ga.at[y2, c], ga.at[y2, c], ss_d.at[i], rs_d.at[i], sib)

    def expand(y2, c2):
        m = y2 * 2 + c2
        r0, r1 = infot[m, :, 0:1], infot[m, :, 1:2]
        for kind in range(3):
            g0 = ga[y2, c2, :, kind * 128 : (kind + 1) * 128]
            g1 = ga[y2, c2, :, (3 + kind) * 128 : (4 + kind) * 128]
            for e in range(8):
                v = jnp.where(r0 == float(e), g0, jnp.where(r1 == float(e), g1, 0.0))
                h, l = split(v)
                gd[0, kind, member_rows(y2, c2), e * 128 : (e + 1) * 128] = h
                gd[1, kind, member_rows(y2, c2), e * 128 : (e + 1) * 128] = l

    spread(0).start()
    spread(1).start()
    pass_on(3, y).start()
    expand(y, c)
    for h in range(2):
        y2 = (y + 3 + 2 * h) % 4
        ref = ga.at[y2, c]
        remote(ref, ref, ss_c.at[h], rs_c.at[h], ym if h else yp).wait_recv()
        spread_half(h, y2).start()
        pass_on(h, y2).start()
    arrived = remote(ga.at[y, 1 - c], ga.at[y, 1 - c], ss_d.at[3], rs_d.at[3], sib)
    arrived.wait_recv()
    expand(y, 1 - c)
    for h in range(2):
        expand((y + 3 + 2 * h) % 4, c)
    far = (y + 2) % 4
    spread_half(0, y + 2).wait_recv()
    spread_half(1, y + 2).wait_recv()
    pass_on(2, far).start()
    for h in range(2):
        y2 = (y + 3 + 2 * h) % 4
        remote(ga.at[y2, 1 - c], ga.at[y2, 1 - c], ss_d.at[h], rs_d.at[h], sib).wait_recv()
        expand(y2, 1 - c)
    expand(far, c)
    remote(ga.at[far, 1 - c], ga.at[far, 1 - c], ss_d.at[2], rs_d.at[2], sib).wait_recv()
    expand(far, 1 - c)
    for i in range(4):
        first(0, i).wait_send()
        first(1, i).wait_send()
        pass_on(i, y).wait_send()
    for h in range(2):
        for p in range(2):
            ring_half(p, h).wait_send()
            ring_full(p, h).wait_send()
        spread(h).wait_send()
        spread_half(h, y).wait_send()
    for cp in cot_out:
        cp.wait_send()

    def weight_grad(xx):
        for kind in range(2):
            wg[kind, :, cols(xx)] = dot3(
                (ttsp[0, 0], ttsp[1, 0]), (gd[0, kind, :, cols(xx)], gd[1, kind, :, cols(xx)]), NN
            )

    def weight_grad_b(q):
        cs = slice(q * 512, q * 512 + 512)
        wg[2, :, cs] = dot3((ttsp[0, 1], ttsp[1, 1]), (gd[0, 2, :, cs], gd[1, 2, :, cs]), NN)

    o = [jnp.where(good, p, q) for p, q in ((zi + 2, hi + 1), (zi + 1, lo - 1), (zi - 1, hi), (zi, lo))]

    def shalf(s, h):
        return remote(
            half(x + 2, o[s], h), xh.at[s, h], ss_t.at[s, h], rs_t.at[s, h], xp if h == 0 else xm
        )

    def sfull(s, h):
        return remote(
            blk(x + 1 - 2 * h, o[s]), xf.at[s, h], ss_q.at[s, h], rs_q.at[s, h], xp if h == 0 else xm
        )

    def by(d, step, q, b, dst):
        return remote(
            chunk(b, q), dst.at[d, :, pl.ds(q * 512, 512)],
            ss_bz.at[d, step, q], rs_by.at[d, step, q], zm if d else zp,
        )

    def take(d, step, q, b, dst):
        by(d, step, q, b, dst).wait_recv()
        where = (2, rows(b), slice(q * 512, q * 512 + 512))
        wg[where] = wg[where] + dst[d, :, q * 512 : q * 512 + 512]

    weight_grad(x + 2)
    for s in range(4):
        for h in range(2):
            shalf(s, h).start()
    weight_grad_b(0)

    @pl.when(good)
    def _():
        by(0, 0, 0, zi + 2, y0).start()

    @pl.when(bad)
    def _():
        by(1, 0, 0, lo - 1, y1).start()

    weight_grad_b(1)

    @pl.when(good)
    def _():
        by(1, 0, 1, zi + 2, y0).start()

    @pl.when(bad)
    def _():
        by(0, 0, 1, hi + 1, y1).start()

    weight_grad(x + 1)
    weight_grad(x - 1)

    @pl.when(bad)
    def _():
        take(0, 0, 0, hi + 1, y0)
        by(0, 0, 0, hi + 1, y1).start()
        take(1, 0, 1, lo - 1, y0)
        by(1, 0, 1, lo - 1, y1).start()

    for s in range(4):
        for h in range(2):
            shalf(s, h).wait_recv()
            where = (slice(0, 2), rows(o[s]), hcols(x + 1 - 2 * h, h))
            wg[where] = wg[where] + xh[s, h]
            sfull(s, h).start()

    @pl.when(good)
    def _():
        take(0, 0, 1, zi + 1, y1)
        by(0, 1, 1, zi + 1, y2b).start()
        take(1, 0, 0, zi - 1, y1)
        by(1, 1, 0, zi - 1, y2b).start()

    weight_grad(x)

    @pl.when(good)
    def _():
        take(0, 0, 0, zi + 1, y1)
        by(0, 1, 0, zi + 1, y2b).start()
        take(1, 0, 1, zi - 1, y1)
        by(1, 1, 1, zi - 1, y2b).start()

    returns = []

    def token_grad(i):
        y2 = (y + STEPS[i]) % 4
        r = pl.ds(pl.multiple_of(y2 * 256, 256), 256)
        res = dot3((wsp[0, 0], wsp[1, 0]), (gd[0, 0, r, :], gd[1, 0, r, :]), NT)
        res = res + dot3((wsp[0, 1], wsp[1, 1]), (gd[0, 1, r, :], gd[1, 1, r, :]), NT)
        xs[y2 * 2, 0:448, :] = res[:, 0:128]
        xs[y2 * 2 + 1, 0:448, :] = res[:, 128:256]
        for n, (dc, dy) in enumerate(OTHERS):
            if dy == STEPS[i]:
                m = y2 * 2 + (c + dc) % 2
                cp = remote(
                    xs.at[m, pl.ds(0, 448), :], cg.at[me], ss_y.at[n], rs_y.at[n], dev(x, y2, z, c + dc)
                )
                cp.start()
                returns.append(cp)

    def total_x(s):
        sfull(s, 0).wait_recv()
        sfull(s, 1).wait_recv()
        where = (slice(0, 2), rows(o[s]), cols(x))
        wg[where] = wg[where] + xf[s, 0] + xf[s, 1]

    def add(s, v):
        where = (slice(0, 2), rows(o[s]), cols(x))
        wg[where] = wg[where] + v

    def add_half(s, h, v):
        where = (slice(0, 2), rows(o[s]), hcols(x, h))
        wg[where] = wg[where] + v

    def zs(i, src, dst):
        return remote(src, dst, ss_s.at[i], rs_s.at[i], zp if i < 2 else zm)

    def bh(h):
        return remote(bhalf(x + 2, h), yh.at[h], ss_bx.at[h], rs_by2.at[h], xm if h else xp)

    def bf(h):
        return remote(bblk(x + 1 - 2 * h), yf.at[h], ss_bx.at[2 + h], rs_by2.at[2 + h], xm if h else xp)

    token_grad(0)
    total_x(0)

    @pl.when(good)
    def _():
        zs(0, half(x, o[0], 0), zh.at[0]).start()
        zs(2, half(x, o[0], 1), zh.at[1]).start()

    @pl.when(bad)
    def _():
        take(0, 1, 1, hi, y2b)
        by(0, 1, 1, hi, y3).start()
        take(1, 1, 0, lo, y2b)
        by(1, 1, 0, lo, y3).start()

    token_grad(1)

    @pl.when(bad)
    def _():
        zs(0, half(x, o[0], 0), zh.at[0]).wait_recv()
        add_half(0, 0, zh[0])
        zs(0, blk(x, o[0]), z1.at[0]).start()

    total_x(1)

    @pl.when(bad)
    def _():
        zs(2, half(x, o[1], 1), zh.at[1]).wait_recv()
        add_half(1, 1, zh[1])
        zs(2, blk(x, o[1]), z1.at[1]).start()
        take(0, 1, 0, hi, y2b)
        by(0, 1, 0, hi, y3).start()
        take(1, 1, 1, lo, y2b)
        by(1, 1, 1, lo, y3).start()

    token_grad(2)
    token_grad(3)

    @pl.when(good)
    def _():
        zs(0, blk(x, o[1]), z1.at[0]).wait_recv()
        add(1, z1[0])
        zs(1, blk(x, o[1]), z2.at[0]).start()

    total_x(2)

    @pl.when(good)
    def _():
        zs(2, blk(x, o[2]), z1.at[1]).wait_recv()
        add(2, z1[1])
        zs(3, blk(x, o[2]), z2.at[1]).start()
        for q in (0, 1):
            take(0, 1, 1 - q, zi, y3)
            take(1, 1, q, zi, y3)
        bh(0).start()
        bh(1).start()

    @pl.when(bad)
    def _():
        zs(1, blk(x, o[2]), z2.at[0]).wait_recv()
        add(2, z2[0])
        zs(1, blk(x, o[2]), z3.at[0]).start()

    total_x(3)

    @pl.when(bad)
    def _():
        zs(3, blk(x, o[3]), z2.at[1]).wait_recv()
        add(3, z2[1])
        zs(3, blk(x, o[3]), z3.at[1]).start()

    @pl.when(good)
    def _():
        for h in range(2):
            bh(h).wait_recv()
            where = (2, rows(zi), hcols(x + 1 - 2 * h, h))
            wg[where] = wg[where] + yh[h]
            bf(h).start()

    cg[me] = xs[me, 0:448, :]

    for cp in returns:
        cp.wait()
    for j in range(28):
        t = jnp.concatenate([cg[m, to : to + n, :] for m, to, frm, n in PIECES[j]], axis=0)
        out[:, j * 128 : (j + 1) * 128] = t.T

    @pl.when(good)
    def _():
        bf(0).wait_recv()
        bf(1).wait_recv()
        where = (2, rows(zi), cols(x))
        wg[where] = wg[where] + yf[0] + yf[1]
        back_b = remote(bhalf(x, 1 - yl), gout.at[2], ss_p.at[1], rs_p.at[4], partner)
        back_b.start()
        zs(1, blk(x, o[3]), z3.at[0]).wait_recv()
        zs(3, blk(x, o[3]), z3.at[1]).wait_recv()
        add(3, z3[0] + z3[1])
        back = remote(half(x, zi, 1 - yl), gout.at[0:2], ss_p.at[0], rs_p.at[3], partner)
        back.start()
        gout[...] = wg[:, rows(zi), hcols(x, yl)]
        back.wait_send()
        back_b.wait_send()
        zs(0, half(x, o[0], 0), zh.at[0]).wait_send()
        zs(2, half(x, o[0], 1), zh.at[1]).wait_send()
        by(0, 0, 0, zi + 2, y0).wait_send()
        by(1, 0, 1, zi + 2, y0).wait_send()
        for h in range(2):
            bh(h).wait_send()
            bf(h).wait_send()

    @pl.when(bad)
    def _():
        remote(half(x, zi, 1 - yl), gout.at[0:2], ss_p.at[0], rs_p.at[3], partner).wait_recv()
        remote(bhalf(x, 1 - yl), gout.at[2], ss_p.at[1], rs_p.at[4], partner).wait_recv()
        zs(0, blk(x, o[0]), z1.at[0]).wait_send()
        zs(2, blk(x, o[1]), z1.at[1]).wait_send()
        for q in (0, 1):
            by(0, 0, q, hi + 1, y1).wait_send()
            by(1, 0, q, lo - 1, y1).wait_send()

    for q in (0, 1):
        by(0, 1, q, zi, y2b).wait_send()
        by(1, 1, q, zi, y2b).wait_send()
    zs(1, blk(x, o[2]), z3.at[0]).wait_send()
    zs(3, blk(x, o[3]), z3.at[1]).wait_send()
    for s in range(4):
        for h in range(2):
            shalf(s, h).wait_send()
            sfull(s, h).wait_send()


def local(tokens, cotangent, routes, gates, w_gate, w_up, w_down):
    vm = pl.BlockSpec(memory_space=pltpu.VMEM)
    dma = pltpu.SemaphoreType.DMA
    full, hlf = (2, ROWS, 256), (2, ROWS, 128)

    def f32(*shape):
        return pltpu.VMEM(shape, F32)

    def bf16(*shape):
        return pltpu.VMEM(shape, BF16)

    out, gout = pl.pallas_call(
        kernel,
        out_shape=(jax.ShapeDtypeStruct((TOK, 3584), F32), jax.ShapeDtypeStruct((3, ROWS, 128), F32)),
        in_specs=[vm] * 7,
        out_specs=(vm, vm),
        scratch_shapes=[
            f32(8, 456, TOK), f32(8, 448, TOK), f32(8, 456, TOK), f32(8, 448, TOK), f32(3, 448, 1024),
            bf16(2, 3, 448, 1024), bf16(2, 1024, 448), bf16(2, 256, 448), bf16(2, 2, 448, 1024), f32(8, TOK, 8), f32(4, 2, TOK, 768),
            f32(4, TOK, 768), f32(2, 64, 768), f32(2, TOK, 768), f32(4, 2, TOK, 768), bf16(2, 3, 1024, 1024),
            f32(4, 2, *hlf), f32(4, 2, *full),
            f32(2, *hlf), f32(2, *full), f32(2, *full), f32(2, *full),
            f32(2, ROWS, 1024), f32(2, ROWS, 1024), f32(2, ROWS, 1024), f32(2, ROWS, 1024),
            f32(2, ROWS, 128), f32(2, ROWS, 256),
            dma((4,)), dma((4,)), dma((2, 2, 2)), dma((2, 2, 2)), dma((2, 2, 2)), dma((4,)),
            dma((5,)), dma((7,)), dma((7,)), dma((7,)), dma((7,)), dma((4,)), dma((5,)), dma((4,)), dma((4,)),
            dma((4, 4)), dma((4, 4)),
            dma((2, 4)), dma((2, 4)), dma((2, 4)), dma((2, 4)), dma((4,)), dma((4,)), dma((4,)), dma((4,)),
            dma((4, 2)), dma((4, 2)), dma((4, 2)), dma((4, 2)), dma((7,)), dma((7,)), dma((4,)), dma((4,)),
        ],
        compiler_params=pltpu.CompilerParams(
            collective_id=0, has_side_effects=True, vmem_limit_bytes=VMEM_LIMIT
        ),
        cost_estimate=pl.CostEstimate(flops=20_000_000_000, bytes_accessed=8_000_000, transcendentals=40_000),
    )(tokens, cotangent, routes.T, gates.T, w_gate[0], w_up[0], w_down[0])
    return out, gout[0:1], gout[1:2], gout[2:3]


def solution(mesh):
    rows = P(("dp", "expert"), None)
    weights = P("expert", "dp", None)
    return jax.shard_map(
        local,
        mesh=mesh,
        in_specs=(rows, rows, rows, rows, weights, weights, weights),
        out_specs=(rows, weights, weights, weights),
        check_vma=False,
    )
```

```python
import jax
import jax.numpy as jnp
from jax import lax
from jax.experimental import pallas as pl
from jax.experimental.pallas import tpu as pltpu
from jax.sharding import PartitionSpec as P

MESH = pl.DeviceIdType.MESH
VMEM_LIMIT = 62 * 2**20
ROWS = 112
TOK = 128
F32 = jnp.float32
BF16 = jnp.bfloat16
NN = (((1,), (0,)), ((), ()))
NT = (((1,), (1,)), ((), ()))


def coords():
    dp = lax.axis_index("dp")
    e = lax.axis_index("expert")
    return e // 2, (dp // 16) * 2 + e % 2, (dp // 2) % 8, dp % 2


def dev(x, y, z, c):
    x, y, z, c = (x + 4) % 4, (y + 4) % 4, (z + 8) % 8, c % 2
    return ((y // 2) * 8 + z) * 2 + c, x * 2 + y % 2


def remote(src, dst, ss, rs, to):
    return pltpu.make_async_remote_copy(
        src_ref=src, dst_ref=dst, send_sem=ss, recv_sem=rs, device_id=to, device_id_type=MESH
    )


def greet(peers):
    bar = pltpu.get_barrier_semaphore()
    for p in peers:
        pl.semaphore_signal(bar, 1, device_id=p, device_id_type=MESH)
    pl.semaphore_wait(bar, len(peers))


def split(v):
    hi = v.astype(BF16)
    return hi, (v - hi.astype(F32)).astype(BF16)


def dot3(a, b, dims):
    def d(p, q):
        return lax.dot_general(p, q, dims, preferred_element_type=F32)

    return d(a[0], b[0]) + d(a[0], b[1]) + d(a[1], b[0])


PIECES = []
for j in range(28):
    r = j * 128
    found = []
    while r < j * 128 + 128:
        shard = r // ROWS
        stop = min((shard + 1) * ROWS, j * 128 + 128)
        yh, zz, cc = shard // 16, (shard // 2) % 8, shard % 2
        member = (yh * 2 + zz % 2) * 2 + cc
        found.append((member, (zz // 2) * ROWS + r - shard * ROWS, r - j * 128, stop - r))
        r = stop
    PIECES.append(found)

OTHERS = [(dc, dy) for dy in (2, 1, 3, 0) for dc in (0, 1) if (dc, dy) != (0, 0)]


def kernel(
    tok, cot, route, gate, w0, w1, w2, out, gout,
    tokv, cotv, xs, xc, xg, cg, wg, wsp, tsp, csp, ttsp, infot, part, buf, got_h, got, ga, gd, xh, xf, zh, z1, z2, z3,
    y0, y1, y2b, y3, yh, yf, ss_bx, rs_bx, ss_bz, rs_bz, rs_by, rs_by2,
    s_l, ss_x, rs_x, ss_xc, rs_xc, ss_p, rs_p, ss_z, rs_z, ss_r, rs_r,
    ss_a, rs_a, ss_b, rs_b, ss_c, rs_c, ss_d, rs_d,
    ss_t, rs_t, ss_q, rs_q, ss_y, rs_y, ss_s, rs_s,
):
    x, y, z, c = coords()
    yl = y % 2
    good = (z % 2) == yl
    bad = jnp.logical_not(good)
    me = y * 2 + c
    zi = z // 2
    zp, zm = dev(x, y, z + 1, c), dev(x, y, z - 1, c)
    xp, xm = dev(x + 1, y, z, c), dev(x - 1, y, z, c)
    partner = dev(x, (y // 2) * 2 + 1 - yl, z, c)
    sib = dev(x, y, z, 1 - c)
    load_t = pltpu.make_async_copy(tok, tokv, s_l.at[5])
    load_c = pltpu.make_async_copy(cot, cotv, s_l.at[6])
    load_t.start()
    load_c.start()
    greet([dev(x, y + dy, z, c + dc) for dc, dy in OTHERS] + [zp, zm, xp, xm])

    def rows(b):
        return pl.ds(pl.multiple_of(((b + 4) % 4) * ROWS, 16), ROWS)

    def cols(xx):
        return pl.ds(pl.multiple_of(((xx + 4) % 4) * 256, 256), 256)

    def hcols(xx, h):
        return pl.ds(pl.multiple_of(((xx + 4) % 4) * 256 + h * 128, 128), 128)

    def blk(xx, b):
        return wg.at[0:2, rows(b), cols(xx)]

    def half(xx, b, h):
        return wg.at[0:2, rows(b), hcols(xx, h)]

    def chunk(b, q):
        return wg.at[2, rows(b), pl.ds(q * 512, 512)]

    def bblk(xx):
        return wg.at[2, rows(zi), cols(xx)]

    def bhalf(xx, h):
        return wg.at[2, rows(zi), hcols(xx, h)]

    ws = (w0, w1, w2)
    local = [pltpu.make_async_copy(ws[k], wg.at[k, rows(zi), hcols(x, yl)], s_l.at[k]) for k in range(3)]
    shift = [
        remote(ws[k], wg.at[k, rows(zi), hcols(x, yl)], ss_p.at[k], rs_p.at[k], partner) for k in range(3)
    ]

    @pl.when(good)
    def _():
        for cp in local:
            cp.start()

    @pl.when(bad)
    def _():
        for cp in shift:
            cp.start()

    facts = jnp.concatenate([route[...].astype(F32), gate[...], jnp.zeros((4, TOK), F32)], axis=0)
    for m in range(8):
        xs[m, 448:456, :] = facts

    def transpose(ref, dst):
        for j in range(28):
            t = ref[:, j * 128 : (j + 1) * 128].T
            for m, to, frm, n in PIECES[j]:
                dst[m, to : to + n, :] = t[frm : frm + n]

    def group(src, dst, ss, rs):
        cps = []
        for i, (dc, dy) in enumerate(OTHERS):
            y2, c2 = (y + dy) % 4, (c + dc) % 2
            cps.append(remote(src.at[y2 * 2 + c2], dst.at[me], ss.at[i], rs.at[i], dev(x, y2, z, c2)))
        return cps

    load_t.wait()
    transpose(tokv, xs)
    keep = pltpu.make_async_copy(xs.at[me], xg.at[me], s_l.at[3])
    keep.start()
    tokens_out = group(xs, xg, ss_x, rs_x)
    for cp in tokens_out:
        cp.start()

    def member_rows(y2, c2):
        return pl.ds(pl.multiple_of(y2 * 256 + c2 * 128, 128), 128)

    def prepare_t(y2):
        for c2 in range(2):
            m = y2 * 2 + c2
            infot[m, :, 0:8] = xg[m, 448:456, :].T
            v = xg[m, 0:448, :]
            r = member_rows(y2, c2)
            ttsp[0, 0, :, r], ttsp[1, 0, :, r] = split(v)
            tsp[0, r, :], tsp[1, r, :] = split(v.T)

    def prepare_c(y2):
        for c2 in range(2):
            v = cg[y2 * 2 + c2]
            r = member_rows(y2, c2)
            ttsp[0, 1, :, r], ttsp[1, 1, :, r] = split(v)
            csp[0, c2 * 128 : (c2 + 1) * 128, :], csp[1, c2 * 128 : (c2 + 1) * 128, :] = split(v.T)

    lo = (z - 1 - yl + 8) // 2
    hi = lo + 1
    b0 = jnp.where(good, zi, lo)
    b1 = jnp.where(good, zi - 1, hi)
    b2 = jnp.where(good, zi + 1, lo - 1)
    b3 = jnp.where(good, zi + 2, hi + 1)

    def zcp(i, ref, to):
        return remote(ref, ref, ss_z.at[i], rs_z.at[i], to)

    def xcp(s, i, ref):
        return remote(ref, ref, ss_r.at[s, i], rs_r.at[s, i], xp if i % 2 == 0 else xm)

    def start_x(s, b):
        xcp(s, 0, blk(x, b)).start()
        xcp(s, 1, blk(x, b)).start()

    def forward_x(s, b):
        xcp(s, 0, blk(x - 1, b)).wait_recv()
        xcp(s, 2, half(x - 1, b, 0)).start()
        xcp(s, 1, blk(x + 1, b)).wait_recv()
        xcp(s, 3, half(x + 1, b, 1)).start()

    def finish_x(s, b):
        xcp(s, 2, half(x - 2, b, 0)).wait_recv()
        xcp(s, 3, half(x + 2, b, 1)).wait_recv()
        for i in range(4):
            (xcp(s, i, blk(x, b)) if i < 2 else xcp(s, i, half(x, b, 0))).wait_send()

    def bx(i, ref):
        return remote(ref, ref, ss_bx.at[i], rs_bx.at[i], xp if i % 2 == 0 else xm)

    def bz(d, step, q, b):
        return remote(
            chunk(b, q), chunk(b, q), ss_bz.at[d, step, q], rs_bz.at[d, step, q], zm if d else zp
        )

    @pl.when(good)
    def _():
        for k in range(3):
            local[k].wait()
            remote(ws[k], wg.at[k, rows(zi), hcols(x, 1 - yl)], ss_p.at[k], rs_p.at[k], partner).wait_recv()
        zcp(0, blk(x, b0), zp).start()
        zcp(2, blk(x, b0), zm).start()
        bx(0, bblk(x)).start()
        bx(1, bblk(x)).start()
        start_x(0, b0)

    load_c.wait()
    transpose(cotv, xc)
    keep_c = pltpu.make_async_copy(xc.at[me], cg.at[me], s_l.at[4])
    keep_c.start()
    cot_out = group(xc, cg, ss_xc, rs_xc)
    for cp in cot_out:
        cp.start()

    @pl.when(good)
    def _():
        bx(0, bblk(x - 1)).wait_recv()
        bx(2, bhalf(x - 1, 0)).start()
        bx(1, bblk(x + 1)).wait_recv()
        bx(3, bhalf(x + 1, 1)).start()
        bx(2, bhalf(x - 2, 0)).wait_recv()
        bx(3, bhalf(x + 2, 1)).wait_recv()
        for q in (0, 1):
            bz(0, 0, q, b0).start()
            bz(1, 0, 1 - q, b0).start()

    @pl.when(bad)
    def _():
        zcp(0, blk(x, b0), zp).wait_recv()
        zcp(0, blk(x, b0), zp).start()
        start_x(0, b0)
        zcp(2, blk(x, b1), zm).wait_recv()
        zcp(2, blk(x, b1), zm).start()
        start_x(1, b1)

    forward_x(0, b0)

    @pl.when(good)
    def _():
        zcp(0, blk(x, b1), zp).wait_recv()
        zcp(1, blk(x, b1), zp).start()
        start_x(1, b1)
        zcp(2, blk(x, b2), zm).wait_recv()
        zcp(3, blk(x, b2), zm).start()
        start_x(2, b2)

    @pl.when(bad)
    def _():
        for q in (0, 1):
            bz(0, 0, q, b0).wait_recv()
            bz(0, 0, q, b0).start()
            bz(1, 0, 1 - q, b1).wait_recv()
            bz(1, 0, 1 - q, b1).start()

    forward_x(1, b1)

    @pl.when(bad)
    def _():
        zcp(1, blk(x, b2), zp).wait_recv()
        zcp(1, half(x, b2, 0), zp).start()
        start_x(2, b2)
        zcp(3, blk(x, b3), zm).wait_recv()
        zcp(3, half(x, b3, 1), zm).start()
        start_x(3, b3)

    @pl.when(good)
    def _():
        for q in (0, 1):
            bz(0, 0, q, b1).wait_recv()
            bz(0, 1, q, b1).start()
            bz(1, 0, 1 - q, b2).wait_recv()
            bz(1, 1, 1 - q, b2).start()

    keep.wait()
    for cp in tokens_out:
        cp.wait_recv()
    prepare_t(y)
    prepare_t((y + 1) % 4)
    forward_x(2, b2)
    prepare_t((y + 2) % 4)
    prepare_t((y + 3) % 4)

    @pl.when(good)
    def _():
        zcp(1, half(x, b3, 0), zp).wait_recv()
        zcp(3, half(x, b3, 1), zm).wait_recv()
        start_x(3, b3)

    @pl.when(bad)
    def _():
        bz(0, 1, 0, b2).wait_recv()
        bz(0, 1, 0, b2).start()
        bz(1, 1, 1, b3).wait_recv()
        bz(1, 1, 1, b3).start()
        bz(0, 1, 1, b2).wait_recv()
        bz(1, 1, 0, b3).wait_recv()

    forward_x(3, b3)
    for s, b in enumerate((b0, b1, b2, b3)):
        finish_x(s, b)
    zcp(0, blk(x, b0), zp).wait_send()
    zcp(2, blk(x, b0), zm).wait_send()
    for q in (0, 1):
        bz(0, 0, q, b0).wait_send()
        bz(1, 0, q, b0).wait_send()
    bz(0, 1, 0, b0).wait_send()
    bz(1, 1, 1, b0).wait_send()

    @pl.when(good)
    def _():
        bz(0, 1, 0, b3).wait_recv()
        bz(1, 1, 1, b3).wait_recv()
        zcp(1, blk(x, b1), zp).wait_send()
        zcp(3, blk(x, b1), zm).wait_send()
        bz(0, 1, 1, b1).wait_send()
        bz(1, 1, 0, b1).wait_send()
        for i in range(4):
            bx(i, bblk(x) if i < 2 else bhalf(x, 0)).wait_send()

    @pl.when(bad)
    def _():
        zcp(1, half(x, b1, 0), zp).wait_send()
        zcp(3, half(x, b1, 1), zm).wait_send()
        for cp in shift:
            cp.wait_send()

    for cp in tokens_out:
        cp.wait_send()
    def split_w(kinds):
        def step(i, _):
            r = pl.ds(pl.multiple_of(i * 32, 32), 32)
            for k in kinds:
                h, l = split(wg[k, r, :])
                wsp[0, k, r, :] = h
                wsp[1, k, r, :] = l
            return 0

        lax.fori_loop(0, 14, step, 0)

    def forward(y2, kinds):
        r = [
            jnp.concatenate([infot[y2 * 2, :, k : k + 1], infot[y2 * 2 + 1, :, k : k + 1]], axis=0)
            for k in range(2)
        ]
        rr = pl.ds(pl.multiple_of(y2 * 256, 256), 256)
        for kind in kinds:
            t = (csp[0], csp[1]) if kind == 2 else (tsp[0, rr, :], tsp[1, rr, :])
            sel = [jnp.zeros((256, 128), F32)] * 2
            for q in range(4):
                cs = slice(q * 256, (q + 1) * 256)
                res = dot3(t, (wsp[0, kind, :, cs], wsp[1, kind, :, cs]), NN)
                for e in range(2):
                    for k in range(2):
                        sel[k] = jnp.where(r[k] == float(q * 2 + e), res[:, e * 128 : (e + 1) * 128], sel[k])
            for k in range(2):
                base = (kind * 2 + k) * 128
                part[y2, 0, :, base : base + 128] = sel[k][0:128]
                part[y2, 1, :, base : base + 128] = sel[k][128:256]

    STEPS = (2, 1, 3, 0)
    COLS = (pl.ds(0, 512), pl.ds(512, 256))

    def first(p, i):
        y2 = (y + STEPS[i]) % 4
        return remote(
            part.at[y2, 1 - c, :, COLS[p]], buf.at[y2, :, COLS[p]], ss_a.at[p, i], rs_a.at[p, i], sib
        )

    yp, ym = dev(x, y + 1, z, c), dev(x, y - 1, z, c)

    def ring_half(p, h):
        return remote(
            buf.at[(y + 2) % 4, pl.ds(64 * h, 64), COLS[p]], got_h.at[h, :, COLS[p]],
            ss_b.at[p, h], rs_b.at[p, h], ym if h else yp,
        )

    def ring_full(p, h):
        return remote(
            buf.at[(y + 1 + 2 * h) % 4, :, COLS[p]], got.at[h, :, COLS[p]],
            ss_b.at[p, 2 + h], rs_b.at[p, 2 + h], ym if h else yp,
        )

    def merge(p, i):
        y2 = (y + STEPS[i]) % 4
        first(p, i).wait_recv()
        buf[y2, :, COLS[p]] = buf[y2, :, COLS[p]] + part[y2, c, :, COLS[p]]
        if i == 0:
            ring_half(p, 0).start()
            ring_half(p, 1).start()
        elif i < 3:
            h = i - 1
            ring_half(p, h).wait_recv()
            r = pl.ds(64 * h, 64)
            buf[y2, r, COLS[p]] = buf[y2, r, COLS[p]] + got_h[h, :, COLS[p]]
            ring_full(p, h).start()

    split_w((0, 1))
    for i in range(4):
        forward((y + STEPS[i]) % 4, (0, 1))
        first(0, i).start()
        if i == 1:
            merge(0, 0)
    split_w((2,))
    merge(0, 1)
    keep_c.wait()
    for i in range(4):
        y2 = (y + STEPS[i]) % 4
        for n, (dc, dy) in enumerate(OTHERS):
            if (4 - dy) % 4 == STEPS[i]:
                cot_out[n].wait_recv()
        prepare_c(y2)
        forward(y2, (2,))
        first(1, i).start()
        if i == 0:
            merge(0, 2)
            merge(0, 3)
        else:
            merge(1, i - 1)
    merge(1, 3)
    for p in range(2):
        for h in range(2):
            ring_full(p, h).wait_recv()
    total = buf[y] + got[0] + got[1]

    for k in range(2):
        g = infot[me, :, 2 + k : 3 + k]
        base = k * 384
        pre_gate = total[:, k * 128 : k * 128 + 128]
        pre_up = total[:, k * 128 + 256 : k * 128 + 384]
        back = total[:, k * 128 + 512 : k * 128 + 640] * g
        s = jax.nn.sigmoid(pre_gate)
        activated = pre_gate * s
        slopes = s * (1.0 + pre_gate * (1.0 - s))
        ga[y, c, :, base : base + 128] = back * pre_up * slopes
        ga[y, c, :, base + 128 : base + 256] = back * activated
        ga[y, c, :, base + 256 : base + 384] = activated * pre_up * g

    def spread(h):
        return remote(ga.at[y, c], ga.at[y, c], ss_c.at[h], rs_c.at[h], ym if h else yp)

    def spread_half(h, y2):
        ref = ga.at[y2 % 4, c, pl.ds(64 * h, 64), :]
        return remote(ref, ref, ss_c.at[2 + h], rs_c.at[2 + h], ym if h else yp)

    def pass_on(i, y2):
        return remote(ga.at[y2, c], ga.at[y2, c], ss_d.at[i], rs_d.at[i], sib)

    def expand(y2, c2):
        m = y2 * 2 + c2
        r0, r1 = infot[m, :, 0:1], infot[m, :, 1:2]
        for kind in range(3):
            g0 = ga[y2, c2, :, kind * 128 : (kind + 1) * 128]
            g1 = ga[y2, c2, :, (3 + kind) * 128 : (4 + kind) * 128]
            for e in range(8):
                v = jnp.where(r0 == float(e), g0, jnp.where(r1 == float(e), g1, 0.0))
                h, l = split(v)
                gd[0, kind, member_rows(y2, c2), e * 128 : (e + 1) * 128] = h
                gd[1, kind, member_rows(y2, c2), e * 128 : (e + 1) * 128] = l

    spread(0).start()
    spread(1).start()
    pass_on(3, y).start()
    expand(y, c)
    for h in range(2):
        y2 = (y + 3 + 2 * h) % 4
        ref = ga.at[y2, c]
        remote(ref, ref, ss_c.at[h], rs_c.at[h], ym if h else yp).wait_recv()
        spread_half(h, y2).start()
        pass_on(h, y2).start()
    arrived = remote(ga.at[y, 1 - c], ga.at[y, 1 - c], ss_d.at[3], rs_d.at[3], sib)
    arrived.wait_recv()
    expand(y, 1 - c)
    for h in range(2):
        expand((y + 3 + 2 * h) % 4, c)
    far = (y + 2) % 4
    spread_half(0, y + 2).wait_recv()
    spread_half(1, y + 2).wait_recv()
    pass_on(2, far).start()
    for h in range(2):
        y2 = (y + 3 + 2 * h) % 4
        remote(ga.at[y2, 1 - c], ga.at[y2, 1 - c], ss_d.at[h], rs_d.at[h], sib).wait_recv()
        expand(y2, 1 - c)
    expand(far, c)
    remote(ga.at[far, 1 - c], ga.at[far, 1 - c], ss_d.at[2], rs_d.at[2], sib).wait_recv()
    expand(far, 1 - c)
    for i in range(4):
        first(0, i).wait_send()
        first(1, i).wait_send()
        pass_on(i, y).wait_send()
    for h in range(2):
        for p in range(2):
            ring_half(p, h).wait_send()
            ring_full(p, h).wait_send()
        spread(h).wait_send()
        spread_half(h, y).wait_send()
    for cp in cot_out:
        cp.wait_send()

    def weight_grad(xx):
        for kind in range(2):
            wg[kind, :, cols(xx)] = dot3(
                (ttsp[0, 0], ttsp[1, 0]), (gd[0, kind, :, cols(xx)], gd[1, kind, :, cols(xx)]), NN
            )

    def weight_grad_b(q):
        cs = slice(q * 512, q * 512 + 512)
        wg[2, :, cs] = dot3((ttsp[0, 1], ttsp[1, 1]), (gd[0, 2, :, cs], gd[1, 2, :, cs]), NN)

    o = [jnp.where(good, p, q) for p, q in ((zi + 2, hi + 1), (zi + 1, lo - 1), (zi - 1, hi), (zi, lo))]

    def shalf(s, h):
        return remote(
            half(x + 2, o[s], h), xh.at[s, h], ss_t.at[s, h], rs_t.at[s, h], xp if h == 0 else xm
        )

    def sfull(s, h):
        return remote(
            blk(x + 1 - 2 * h, o[s]), xf.at[s, h], ss_q.at[s, h], rs_q.at[s, h], xp if h == 0 else xm
        )

    def by(d, step, q, b, dst):
        return remote(
            chunk(b, q), dst.at[d, :, pl.ds(q * 512, 512)],
            ss_bz.at[d, step, q], rs_by.at[d, step, q], zm if d else zp,
        )

    def take(d, step, q, b, dst):
        by(d, step, q, b, dst).wait_recv()
        where = (2, rows(b), slice(q * 512, q * 512 + 512))
        wg[where] = wg[where] + dst[d, :, q * 512 : q * 512 + 512]

    weight_grad(x + 2)
    for s in range(4):
        for h in range(2):
            shalf(s, h).start()
    weight_grad_b(0)

    @pl.when(good)
    def _():
        by(0, 0, 0, zi + 2, y0).start()

    @pl.when(bad)
    def _():
        by(1, 0, 0, lo - 1, y1).start()

    weight_grad_b(1)

    @pl.when(good)
    def _():
        by(1, 0, 1, zi + 2, y0).start()

    @pl.when(bad)
    def _():
        by(0, 0, 1, hi + 1, y1).start()

    weight_grad(x + 1)
    weight_grad(x - 1)

    @pl.when(bad)
    def _():
        take(0, 0, 0, hi + 1, y0)
        by(0, 0, 0, hi + 1, y1).start()
        take(1, 0, 1, lo - 1, y0)
        by(1, 0, 1, lo - 1, y1).start()

    for s in range(4):
        for h in range(2):
            shalf(s, h).wait_recv()
            where = (slice(0, 2), rows(o[s]), hcols(x + 1 - 2 * h, h))
            wg[where] = wg[where] + xh[s, h]
            sfull(s, h).start()

    @pl.when(good)
    def _():
        take(0, 0, 1, zi + 1, y1)
        by(0, 1, 1, zi + 1, y2b).start()
        take(1, 0, 0, zi - 1, y1)
        by(1, 1, 0, zi - 1, y2b).start()

    weight_grad(x)

    @pl.when(good)
    def _():
        take(0, 0, 0, zi + 1, y1)
        by(0, 1, 0, zi + 1, y2b).start()
        take(1, 0, 1, zi - 1, y1)
        by(1, 1, 1, zi - 1, y2b).start()

    returns = []

    def token_grad(i):
        y2 = (y + STEPS[i]) % 4
        r = pl.ds(pl.multiple_of(y2 * 256, 256), 256)
        res = dot3((wsp[0, 0], wsp[1, 0]), (gd[0, 0, r, :], gd[1, 0, r, :]), NT)
        res = res + dot3((wsp[0, 1], wsp[1, 1]), (gd[0, 1, r, :], gd[1, 1, r, :]), NT)
        xs[y2 * 2, 0:448, :] = res[:, 0:128]
        xs[y2 * 2 + 1, 0:448, :] = res[:, 128:256]
        for n, (dc, dy) in enumerate(OTHERS):
            if dy == STEPS[i]:
                m = y2 * 2 + (c + dc) % 2
                cp = remote(
                    xs.at[m, pl.ds(0, 448), :], cg.at[me], ss_y.at[n], rs_y.at[n], dev(x, y2, z, c + dc)
                )
                cp.start()
                returns.append(cp)

    def total_x(s):
        sfull(s, 0).wait_recv()
        sfull(s, 1).wait_recv()
        where = (slice(0, 2), rows(o[s]), cols(x))
        wg[where] = wg[where] + xf[s, 0] + xf[s, 1]

    def add(s, v):
        where = (slice(0, 2), rows(o[s]), cols(x))
        wg[where] = wg[where] + v

    def add_half(s, h, v):
        where = (slice(0, 2), rows(o[s]), hcols(x, h))
        wg[where] = wg[where] + v

    def zs(i, src, dst):
        return remote(src, dst, ss_s.at[i], rs_s.at[i], zp if i < 2 else zm)

    def bh(h):
        return remote(bhalf(x + 2, h), yh.at[h], ss_bx.at[h], rs_by2.at[h], xm if h else xp)

    def bf(h):
        return remote(bblk(x + 1 - 2 * h), yf.at[h], ss_bx.at[2 + h], rs_by2.at[2 + h], xm if h else xp)

    token_grad(0)
    total_x(0)

    @pl.when(good)
    def _():
        zs(0, half(x, o[0], 0), zh.at[0]).start()
        zs(2, half(x, o[0], 1), zh.at[1]).start()

    @pl.when(bad)
    def _():
        take(0, 1, 1, hi, y2b)
        by(0, 1, 1, hi, y3).start()
        take(1, 1, 0, lo, y2b)
        by(1, 1, 0, lo, y3).start()

    token_grad(1)

    @pl.when(bad)
    def _():
        zs(0, half(x, o[0], 0), zh.at[0]).wait_recv()
        add_half(0, 0, zh[0])
        zs(0, blk(x, o[0]), z1.at[0]).start()

    total_x(1)

    @pl.when(bad)
    def _():
        zs(2, half(x, o[1], 1), zh.at[1]).wait_recv()
        add_half(1, 1, zh[1])
        zs(2, blk(x, o[1]), z1.at[1]).start()
        take(0, 1, 0, hi, y2b)
        by(0, 1, 0, hi, y3).start()
        take(1, 1, 1, lo, y2b)
        by(1, 1, 1, lo, y3).start()

    token_grad(2)
    token_grad(3)

    @pl.when(good)
    def _():
        zs(0, blk(x, o[1]), z1.at[0]).wait_recv()
        add(1, z1[0])
        zs(1, blk(x, o[1]), z2.at[0]).start()

    total_x(2)

    @pl.when(good)
    def _():
        zs(2, blk(x, o[2]), z1.at[1]).wait_recv()
        add(2, z1[1])
        zs(3, blk(x, o[2]), z2.at[1]).start()
        for q in (0, 1):
            take(0, 1, 1 - q, zi, y3)
            take(1, 1, q, zi, y3)
        bh(0).start()
        bh(1).start()

    @pl.when(bad)
    def _():
        zs(1, blk(x, o[2]), z2.at[0]).wait_recv()
        add(2, z2[0])
        zs(1, blk(x, o[2]), z3.at[0]).start()

    total_x(3)

    @pl.when(bad)
    def _():
        zs(3, blk(x, o[3]), z2.at[1]).wait_recv()
        add(3, z2[1])
        zs(3, blk(x, o[3]), z3.at[1]).start()

    @pl.when(good)
    def _():
        for h in range(2):
            bh(h).wait_recv()
            where = (2, rows(zi), hcols(x + 1 - 2 * h, h))
            wg[where] = wg[where] + yh[h]
            bf(h).start()

    cg[me] = xs[me, 0:448, :]

    for cp in returns:
        cp.wait()
    for j in range(28):
        t = jnp.concatenate([cg[m, to : to + n, :] for m, to, frm, n in PIECES[j]], axis=0)
        tokv[:, j * 128 : (j + 1) * 128] = t.T
    leave = pltpu.make_async_copy(tokv, out, s_l.at[5])
    leave.start()

    @pl.when(good)
    def _():
        bf(0).wait_recv()
        bf(1).wait_recv()
        where = (2, rows(zi), cols(x))
        wg[where] = wg[where] + yf[0] + yf[1]
        back_b = remote(bhalf(x, 1 - yl), gout.at[2], ss_p.at[1], rs_p.at[4], partner)
        back_b.start()
        zs(1, blk(x, o[3]), z3.at[0]).wait_recv()
        zs(3, blk(x, o[3]), z3.at[1]).wait_recv()
        add(3, z3[0] + z3[1])
        back = remote(half(x, zi, 1 - yl), gout.at[0:2], ss_p.at[0], rs_p.at[3], partner)
        back.start()
        gout[...] = wg[:, rows(zi), hcols(x, yl)]
        back.wait_send()
        back_b.wait_send()
        zs(0, half(x, o[0], 0), zh.at[0]).wait_send()
        zs(2, half(x, o[0], 1), zh.at[1]).wait_send()
        by(0, 0, 0, zi + 2, y0).wait_send()
        by(1, 0, 1, zi + 2, y0).wait_send()
        for h in range(2):
            bh(h).wait_send()
            bf(h).wait_send()

    @pl.when(bad)
    def _():
        remote(half(x, zi, 1 - yl), gout.at[0:2], ss_p.at[0], rs_p.at[3], partner).wait_recv()
        remote(bhalf(x, 1 - yl), gout.at[2], ss_p.at[1], rs_p.at[4], partner).wait_recv()
        zs(0, blk(x, o[0]), z1.at[0]).wait_send()
        zs(2, blk(x, o[1]), z1.at[1]).wait_send()
        for q in (0, 1):
            by(0, 0, q, hi + 1, y1).wait_send()
            by(1, 0, q, lo - 1, y1).wait_send()

    for q in (0, 1):
        by(0, 1, q, zi, y2b).wait_send()
        by(1, 1, q, zi, y2b).wait_send()
    zs(1, blk(x, o[2]), z3.at[0]).wait_send()
    zs(3, blk(x, o[3]), z3.at[1]).wait_send()
    leave.wait()
    for s in range(4):
        for h in range(2):
            shalf(s, h).wait_send()
            sfull(s, h).wait_send()


def local(tokens, cotangent, routes, gates, w_gate, w_up, w_down):
    vm = pl.BlockSpec(memory_space=pltpu.VMEM)
    anyspace = pl.BlockSpec(memory_space=pl.ANY)
    dma = pltpu.SemaphoreType.DMA
    full, hlf = (2, ROWS, 256), (2, ROWS, 128)

    def f32(*shape):
        return pltpu.VMEM(shape, F32)

    def bf16(*shape):
        return pltpu.VMEM(shape, BF16)

    out, gout = pl.pallas_call(
        kernel,
        out_shape=(jax.ShapeDtypeStruct((TOK, 3584), F32), jax.ShapeDtypeStruct((3, ROWS, 128), F32)),
        in_specs=[anyspace] * 2 + [vm] * 5,
        out_specs=(anyspace, vm),
        scratch_shapes=[
            f32(TOK, 3584), f32(TOK, 3584), f32(8, 456, TOK), f32(8, 448, TOK), f32(8, 456, TOK), f32(8, 448, TOK), f32(3, 448, 1024),
            bf16(2, 3, 448, 1024), bf16(2, 1024, 448), bf16(2, 256, 448), bf16(2, 2, 448, 1024), f32(8, TOK, 8), f32(4, 2, TOK, 768),
            f32(4, TOK, 768), f32(2, 64, 768), f32(2, TOK, 768), f32(4, 2, TOK, 768), bf16(2, 3, 1024, 1024),
            f32(4, 2, *hlf), f32(4, 2, *full),
            f32(2, *hlf), f32(2, *full), f32(2, *full), f32(2, *full),
            f32(2, ROWS, 1024), f32(2, ROWS, 1024), f32(2, ROWS, 1024), f32(2, ROWS, 1024),
            f32(2, ROWS, 128), f32(2, ROWS, 256),
            dma((4,)), dma((4,)), dma((2, 2, 2)), dma((2, 2, 2)), dma((2, 2, 2)), dma((4,)),
            dma((7,)), dma((7,)), dma((7,)), dma((7,)), dma((7,)), dma((4,)), dma((5,)), dma((4,)), dma((4,)),
            dma((4, 4)), dma((4, 4)),
            dma((2, 4)), dma((2, 4)), dma((2, 4)), dma((2, 4)), dma((4,)), dma((4,)), dma((4,)), dma((4,)),
            dma((4, 2)), dma((4, 2)), dma((4, 2)), dma((4, 2)), dma((7,)), dma((7,)), dma((4,)), dma((4,)),
        ],
        compiler_params=pltpu.CompilerParams(
            collective_id=0, has_side_effects=True, vmem_limit_bytes=VMEM_LIMIT
        ),
        cost_estimate=pl.CostEstimate(flops=20_000_000_000, bytes_accessed=8_000_000, transcendentals=40_000),
    )(tokens, cotangent, routes.T, gates.T, w_gate[0], w_up[0], w_down[0])
    return out, gout[0:1], gout[1:2], gout[2:3]


def solution(mesh):
    rows = P(("dp", "expert"), None)
    weights = P("expert", "dp", None)
    return jax.shard_map(
        local,
        mesh=mesh,
        in_specs=(rows, rows, rows, rows, weights, weights, weights),
        out_specs=(rows, weights, weights, weights),
        check_vma=False,
    )
```

```python
import jax
import jax.numpy as jnp
from jax import lax
from jax.experimental import pallas as pl
from jax.experimental.pallas import tpu as pltpu
from jax.sharding import PartitionSpec as P

MESH = pl.DeviceIdType.MESH
VMEM_LIMIT = 62 * 2**20
ROWS = 112
TOK = 128
F32 = jnp.float32
BF16 = jnp.bfloat16
NN = (((1,), (0,)), ((), ()))
NT = (((1,), (1,)), ((), ()))


def coords():
    dp = lax.axis_index("dp")
    e = lax.axis_index("expert")
    return e // 2, (dp // 16) * 2 + e % 2, (dp // 2) % 8, dp % 2


def dev(x, y, z, c):
    x, y, z, c = (x + 4) % 4, (y + 4) % 4, (z + 8) % 8, c % 2
    return ((y // 2) * 8 + z) * 2 + c, x * 2 + y % 2


def remote(src, dst, ss, rs, to):
    return pltpu.make_async_remote_copy(
        src_ref=src, dst_ref=dst, send_sem=ss, recv_sem=rs, device_id=to, device_id_type=MESH
    )


def greet(peers):
    bar = pltpu.get_barrier_semaphore()
    for p in peers:
        pl.semaphore_signal(bar, 1, device_id=p, device_id_type=MESH)
    pl.semaphore_wait(bar, len(peers))


def split(v):
    hi = v.astype(BF16)
    return hi, (v - hi.astype(F32)).astype(BF16)


def dot3(a, b, dims):
    def d(p, q):
        return lax.dot_general(p, q, dims, preferred_element_type=F32)

    return d(a[0], b[0]) + d(a[0], b[1]) + d(a[1], b[0])


PIECES = []
for j in range(28):
    r = j * 128
    found = []
    while r < j * 128 + 128:
        shard = r // ROWS
        stop = min((shard + 1) * ROWS, j * 128 + 128)
        yh, zz, cc = shard // 16, (shard // 2) % 8, shard % 2
        member = (yh * 2 + zz % 2) * 2 + cc
        found.append((member, (zz // 2) * ROWS + r - shard * ROWS, r - j * 128, stop - r))
        r = stop
    PIECES.append(found)

OTHERS = [(dc, dy) for dy in (2, 1, 3, 0) for dc in (0, 1) if (dc, dy) != (0, 0)]


def kernel(
    tok, cot, route, gate, w0, w1, w2, out, gout,
    tokv, cotv, xs, xc, xg, cg, wg, wsp, tsp, csp, ttsp, infot, part, buf, got_h, got, ga, gd, xh, xf, zh, z1, z2, z3,
    y0, y1, y2b, y3, yh, yf, ss_bx, rs_bx, ss_bz, rs_bz, rs_by, rs_by2,
    s_l, ss_x, rs_x, ss_xc, rs_xc, ss_p, rs_p, ss_z, rs_z, ss_r, rs_r,
    ss_a, rs_a, ss_b, rs_b, ss_c, rs_c, ss_d, rs_d,
    ss_t, rs_t, ss_q, rs_q, ss_y, rs_y, ss_s, rs_s,
):
    x, y, z, c = coords()
    yl = y % 2
    good = (z % 2) == yl
    bad = jnp.logical_not(good)
    me = y * 2 + c
    zi = z // 2
    zp, zm = dev(x, y, z + 1, c), dev(x, y, z - 1, c)
    xp, xm = dev(x + 1, y, z, c), dev(x - 1, y, z, c)
    partner = dev(x, (y // 2) * 2 + 1 - yl, z, c)
    sib = dev(x, y, z, 1 - c)
    load_t = pltpu.make_async_copy(tok, tokv, s_l.at[5])
    load_c = pltpu.make_async_copy(cot, cotv, s_l.at[6])
    load_t.start()
    load_c.start()
    greet([dev(x, y + dy, z, c + dc) for dc, dy in OTHERS] + [zp, zm, xp, xm])

    def rows(b):
        return pl.ds(pl.multiple_of(((b + 4) % 4) * ROWS, 16), ROWS)

    def cols(xx):
        return pl.ds(pl.multiple_of(((xx + 4) % 4) * 256, 256), 256)

    def hcols(xx, h):
        return pl.ds(pl.multiple_of(((xx + 4) % 4) * 256 + h * 128, 128), 128)

    def blk(xx, b):
        return wg.at[0:2, rows(b), cols(xx)]

    def half(xx, b, h):
        return wg.at[0:2, rows(b), hcols(xx, h)]

    def chunk(b, q):
        return wg.at[2, rows(b), pl.ds(q * 512, 512)]

    def bblk(xx):
        return wg.at[2, rows(zi), cols(xx)]

    def bhalf(xx, h):
        return wg.at[2, rows(zi), hcols(xx, h)]

    ws = (w0, w1, w2)
    local = [pltpu.make_async_copy(ws[k], wg.at[k, rows(zi), hcols(x, yl)], s_l.at[k]) for k in range(3)]
    shift = [
        remote(ws[k], wg.at[k, rows(zi), hcols(x, yl)], ss_p.at[k], rs_p.at[k], partner) for k in range(3)
    ]

    @pl.when(good)
    def _():
        for cp in local:
            cp.start()

    @pl.when(bad)
    def _():
        for cp in shift:
            cp.start()

    facts = jnp.concatenate([route[...].astype(F32), gate[...], jnp.zeros((4, TOK), F32)], axis=0)
    for m in range(8):
        xs[m, 448:456, :] = facts

    def transpose(ref, dst):
        for j in range(28):
            t = ref[:, j * 128 : (j + 1) * 128].T
            for m, to, frm, n in PIECES[j]:
                dst[m, to : to + n, :] = t[frm : frm + n]

    def group(src, dst, ss, rs):
        cps = []
        for i, (dc, dy) in enumerate(OTHERS):
            y2, c2 = (y + dy) % 4, (c + dc) % 2
            cps.append(remote(src.at[y2 * 2 + c2], dst.at[me], ss.at[i], rs.at[i], dev(x, y2, z, c2)))
        return cps

    load_t.wait()
    transpose(tokv, xs)
    keep = pltpu.make_async_copy(xs.at[me], xg.at[me], s_l.at[3])
    keep.start()
    tokens_out = group(xs, xg, ss_x, rs_x)
    for cp in tokens_out:
        cp.start()

    def member_rows(y2, c2):
        return pl.ds(pl.multiple_of(y2 * 256 + c2 * 128, 128), 128)

    def prepare_t(y2):
        for c2 in range(2):
            m = y2 * 2 + c2
            infot[m, :, 0:8] = xg[m, 448:456, :].T
            v = xg[m, 0:448, :]
            r = member_rows(y2, c2)
            ttsp[0, 0, :, r], ttsp[1, 0, :, r] = split(v)
            tsp[0, r, :], tsp[1, r, :] = split(v.T)

    def prepare_c(y2):
        for c2 in range(2):
            v = cg[y2 * 2 + c2]
            r = member_rows(y2, c2)
            ttsp[0, 1, :, r], ttsp[1, 1, :, r] = split(v)
            csp[0, c2 * 128 : (c2 + 1) * 128, :], csp[1, c2 * 128 : (c2 + 1) * 128, :] = split(v.T)

    lo = (z - 1 - yl + 8) // 2
    hi = lo + 1
    b0 = jnp.where(good, zi, lo)
    b1 = jnp.where(good, zi - 1, hi)
    b2 = jnp.where(good, zi + 1, lo - 1)
    b3 = jnp.where(good, zi + 2, hi + 1)

    def zcp(i, ref, to):
        return remote(ref, ref, ss_z.at[i], rs_z.at[i], to)

    def xcp(s, i, ref):
        return remote(ref, ref, ss_r.at[s, i], rs_r.at[s, i], xp if i % 2 == 0 else xm)

    def start_x(s, b):
        xcp(s, 0, blk(x, b)).start()
        xcp(s, 1, blk(x, b)).start()

    def forward_x(s, b):
        xcp(s, 0, blk(x - 1, b)).wait_recv()
        xcp(s, 2, half(x - 1, b, 0)).start()
        xcp(s, 1, blk(x + 1, b)).wait_recv()
        xcp(s, 3, half(x + 1, b, 1)).start()

    def finish_x(s, b):
        xcp(s, 2, half(x - 2, b, 0)).wait_recv()
        xcp(s, 3, half(x + 2, b, 1)).wait_recv()
        for i in range(4):
            (xcp(s, i, blk(x, b)) if i < 2 else xcp(s, i, half(x, b, 0))).wait_send()

    def bx(i, ref):
        return remote(ref, ref, ss_bx.at[i], rs_bx.at[i], xp if i % 2 == 0 else xm)

    def bz(d, step, q, b):
        return remote(
            chunk(b, q), chunk(b, q), ss_bz.at[d, step, q], rs_bz.at[d, step, q], zm if d else zp
        )

    @pl.when(good)
    def _():
        for k in range(3):
            local[k].wait()
            remote(ws[k], wg.at[k, rows(zi), hcols(x, 1 - yl)], ss_p.at[k], rs_p.at[k], partner).wait_recv()
        zcp(0, blk(x, b0), zp).start()
        zcp(2, blk(x, b0), zm).start()
        bx(0, bblk(x)).start()
        bx(1, bblk(x)).start()
        start_x(0, b0)

    load_c.wait()
    transpose(cotv, xc)
    keep_c = pltpu.make_async_copy(xc.at[me], cg.at[me], s_l.at[4])
    keep_c.start()
    cot_out = group(xc, cg, ss_xc, rs_xc)
    for cp in cot_out:
        cp.start()

    @pl.when(good)
    def _():
        bx(0, bblk(x - 1)).wait_recv()
        bx(2, bhalf(x - 1, 0)).start()
        bx(1, bblk(x + 1)).wait_recv()
        bx(3, bhalf(x + 1, 1)).start()
        bx(2, bhalf(x - 2, 0)).wait_recv()
        bx(3, bhalf(x + 2, 1)).wait_recv()
        for q in (0, 1):
            bz(0, 0, q, b0).start()
            bz(1, 0, 1 - q, b0).start()

    @pl.when(bad)
    def _():
        zcp(0, blk(x, b0), zp).wait_recv()
        zcp(0, blk(x, b0), zp).start()
        start_x(0, b0)
        zcp(2, blk(x, b1), zm).wait_recv()
        zcp(2, blk(x, b1), zm).start()
        start_x(1, b1)

    forward_x(0, b0)

    @pl.when(good)
    def _():
        zcp(0, blk(x, b1), zp).wait_recv()
        zcp(1, blk(x, b1), zp).start()
        start_x(1, b1)
        zcp(2, blk(x, b2), zm).wait_recv()
        zcp(3, blk(x, b2), zm).start()
        start_x(2, b2)

    @pl.when(bad)
    def _():
        for q in (0, 1):
            bz(0, 0, q, b0).wait_recv()
            bz(0, 0, q, b0).start()
            bz(1, 0, 1 - q, b1).wait_recv()
            bz(1, 0, 1 - q, b1).start()

    forward_x(1, b1)

    @pl.when(bad)
    def _():
        zcp(1, blk(x, b2), zp).wait_recv()
        zcp(1, half(x, b2, 0), zp).start()
        start_x(2, b2)
        zcp(3, blk(x, b3), zm).wait_recv()
        zcp(3, half(x, b3, 1), zm).start()
        start_x(3, b3)

    @pl.when(good)
    def _():
        for q in (0, 1):
            bz(0, 0, q, b1).wait_recv()
            bz(0, 1, q, b1).start()
            bz(1, 0, 1 - q, b2).wait_recv()
            bz(1, 1, 1 - q, b2).start()

    keep.wait()
    for cp in tokens_out:
        cp.wait_recv()
    prepare_t(y)
    prepare_t((y + 1) % 4)
    forward_x(2, b2)
    prepare_t((y + 2) % 4)
    prepare_t((y + 3) % 4)

    @pl.when(good)
    def _():
        zcp(1, half(x, b3, 0), zp).wait_recv()
        zcp(3, half(x, b3, 1), zm).wait_recv()
        start_x(3, b3)

    @pl.when(bad)
    def _():
        bz(0, 1, 0, b2).wait_recv()
        bz(0, 1, 0, b2).start()
        bz(1, 1, 1, b3).wait_recv()
        bz(1, 1, 1, b3).start()
        bz(0, 1, 1, b2).wait_recv()
        bz(1, 1, 0, b3).wait_recv()

    forward_x(3, b3)
    for s, b in enumerate((b0, b1, b2, b3)):
        finish_x(s, b)
    zcp(0, blk(x, b0), zp).wait_send()
    zcp(2, blk(x, b0), zm).wait_send()
    for q in (0, 1):
        bz(0, 0, q, b0).wait_send()
        bz(1, 0, q, b0).wait_send()
    bz(0, 1, 0, b0).wait_send()
    bz(1, 1, 1, b0).wait_send()

    @pl.when(good)
    def _():
        bz(0, 1, 0, b3).wait_recv()
        bz(1, 1, 1, b3).wait_recv()
        zcp(1, blk(x, b1), zp).wait_send()
        zcp(3, blk(x, b1), zm).wait_send()
        bz(0, 1, 1, b1).wait_send()
        bz(1, 1, 0, b1).wait_send()
        for i in range(4):
            bx(i, bblk(x) if i < 2 else bhalf(x, 0)).wait_send()

    @pl.when(bad)
    def _():
        zcp(1, half(x, b1, 0), zp).wait_send()
        zcp(3, half(x, b1, 1), zm).wait_send()
        for cp in shift:
            cp.wait_send()

    for cp in tokens_out:
        cp.wait_send()
    def split_w(kinds):
        def step(i, _):
            r = pl.ds(pl.multiple_of(i * 32, 32), 32)
            for k in kinds:
                h, l = split(wg[k, r, :])
                wsp[0, k, r, :] = h
                wsp[1, k, r, :] = l
            return 0

        lax.fori_loop(0, 14, step, 0)

    def forward(y2, kinds):
        r = [
            jnp.concatenate([infot[y2 * 2, :, k : k + 1], infot[y2 * 2 + 1, :, k : k + 1]], axis=0)
            for k in range(2)
        ]
        rr = pl.ds(pl.multiple_of(y2 * 256, 256), 256)
        for kind in kinds:
            t = (csp[0], csp[1]) if kind == 2 else (tsp[0, rr, :], tsp[1, rr, :])
            sel = [jnp.zeros((256, 128), F32)] * 2
            for q in range(4):
                cs = slice(q * 256, (q + 1) * 256)
                res = dot3(t, (wsp[0, kind, :, cs], wsp[1, kind, :, cs]), NN)
                for e in range(2):
                    for k in range(2):
                        sel[k] = jnp.where(r[k] == float(q * 2 + e), res[:, e * 128 : (e + 1) * 128], sel[k])
            for k in range(2):
                base = (kind * 2 + k) * 128
                part[y2, 0, :, base : base + 128] = sel[k][0:128]
                part[y2, 1, :, base : base + 128] = sel[k][128:256]

    STEPS = (2, 1, 3, 0)
    COLS = (pl.ds(0, 512), pl.ds(512, 256))

    def first(p, i):
        y2 = (y + STEPS[i]) % 4
        return remote(
            part.at[y2, 1 - c, :, COLS[p]], buf.at[y2, :, COLS[p]], ss_a.at[p, i], rs_a.at[p, i], sib
        )

    yp, ym = dev(x, y + 1, z, c), dev(x, y - 1, z, c)

    def ring_half(p, h):
        return remote(
            buf.at[(y + 2) % 4, pl.ds(64 * h, 64), COLS[p]], got_h.at[h, :, COLS[p]],
            ss_b.at[p, h], rs_b.at[p, h], ym if h else yp,
        )

    def ring_full(p, h):
        return remote(
            buf.at[(y + 1 + 2 * h) % 4, :, COLS[p]], got.at[h, :, COLS[p]],
            ss_b.at[p, 2 + h], rs_b.at[p, 2 + h], ym if h else yp,
        )

    def merge(p, i):
        y2 = (y + STEPS[i]) % 4
        first(p, i).wait_recv()
        buf[y2, :, COLS[p]] = buf[y2, :, COLS[p]] + part[y2, c, :, COLS[p]]
        if i == 0:
            ring_half(p, 0).start()
            ring_half(p, 1).start()
        elif i < 3:
            h = i - 1
            ring_half(p, h).wait_recv()
            r = pl.ds(64 * h, 64)
            buf[y2, r, COLS[p]] = buf[y2, r, COLS[p]] + got_h[h, :, COLS[p]]
            ring_full(p, h).start()

    split_w((0, 1))
    for i in range(4):
        forward((y + STEPS[i]) % 4, (0, 1))
        first(0, i).start()
        if i == 1:
            merge(0, 0)
    split_w((2,))
    merge(0, 1)
    keep_c.wait()
    for i in range(4):
        y2 = (y + STEPS[i]) % 4
        for n, (dc, dy) in enumerate(OTHERS):
            if (4 - dy) % 4 == STEPS[i]:
                cot_out[n].wait_recv()
        prepare_c(y2)
        forward(y2, (2,))
        first(1, i).start()
        if i == 0:
            merge(0, 2)
            merge(0, 3)
        else:
            merge(1, i - 1)
    merge(1, 3)
    for p in range(2):
        for h in range(2):
            ring_full(p, h).wait_recv()
    total = buf[y] + got[0] + got[1]

    for k in range(2):
        g = infot[me, :, 2 + k : 3 + k]
        base = k * 384
        pre_gate = total[:, k * 128 : k * 128 + 128]
        pre_up = total[:, k * 128 + 256 : k * 128 + 384]
        back = total[:, k * 128 + 512 : k * 128 + 640] * g
        s = jax.nn.sigmoid(pre_gate)
        activated = pre_gate * s
        slopes = s * (1.0 + pre_gate * (1.0 - s))
        ga[y, c, :, base : base + 128] = back * pre_up * slopes
        ga[y, c, :, base + 128 : base + 256] = back * activated
        ga[y, c, :, base + 256 : base + 384] = activated * pre_up * g

    def spread(h):
        return remote(ga.at[y, c], ga.at[y, c], ss_c.at[h], rs_c.at[h], ym if h else yp)

    def spread_half(h, y2):
        ref = ga.at[y2 % 4, c, pl.ds(64 * h, 64), :]
        return remote(ref, ref, ss_c.at[2 + h], rs_c.at[2 + h], ym if h else yp)

    def pass_on(i, y2):
        return remote(ga.at[y2, c], ga.at[y2, c], ss_d.at[i], rs_d.at[i], sib)

    def expand(y2, c2):
        m = y2 * 2 + c2
        r0, r1 = infot[m, :, 0:1], infot[m, :, 1:2]
        for kind in range(3):
            g0 = ga[y2, c2, :, kind * 128 : (kind + 1) * 128]
            g1 = ga[y2, c2, :, (3 + kind) * 128 : (4 + kind) * 128]
            for e in range(8):
                v = jnp.where(r0 == float(e), g0, jnp.where(r1 == float(e), g1, 0.0))
                h, l = split(v)
                gd[0, kind, member_rows(y2, c2), e * 128 : (e + 1) * 128] = h
                gd[1, kind, member_rows(y2, c2), e * 128 : (e + 1) * 128] = l

    spread(0).start()
    spread(1).start()
    pass_on(3, y).start()
    expand(y, c)
    for h in range(2):
        y2 = (y + 3 + 2 * h) % 4
        ref = ga.at[y2, c]
        remote(ref, ref, ss_c.at[h], rs_c.at[h], ym if h else yp).wait_recv()
        spread_half(h, y2).start()
        pass_on(h, y2).start()
    arrived = remote(ga.at[y, 1 - c], ga.at[y, 1 - c], ss_d.at[3], rs_d.at[3], sib)
    arrived.wait_recv()
    expand(y, 1 - c)
    for h in range(2):
        expand((y + 3 + 2 * h) % 4, c)
    far = (y + 2) % 4
    spread_half(0, y + 2).wait_recv()
    spread_half(1, y + 2).wait_recv()
    pass_on(2, far).start()
    for h in range(2):
        y2 = (y + 3 + 2 * h) % 4
        remote(ga.at[y2, 1 - c], ga.at[y2, 1 - c], ss_d.at[h], rs_d.at[h], sib).wait_recv()
        expand(y2, 1 - c)
    expand(far, c)
    remote(ga.at[far, 1 - c], ga.at[far, 1 - c], ss_d.at[2], rs_d.at[2], sib).wait_recv()
    expand(far, 1 - c)
    for i in range(4):
        first(0, i).wait_send()
        first(1, i).wait_send()
        pass_on(i, y).wait_send()
    for h in range(2):
        for p in range(2):
            ring_half(p, h).wait_send()
            ring_full(p, h).wait_send()
        spread(h).wait_send()
        spread_half(h, y).wait_send()
    for cp in cot_out:
        cp.wait_send()

    def weight_grad(xx):
        for kind in range(2):
            wg[kind, :, cols(xx)] = dot3(
                (ttsp[0, 0], ttsp[1, 0]), (gd[0, kind, :, cols(xx)], gd[1, kind, :, cols(xx)]), NN
            )

    def weight_grad_b(q):
        cs = slice(q * 512, q * 512 + 512)
        wg[2, :, cs] = dot3((ttsp[0, 1], ttsp[1, 1]), (gd[0, 2, :, cs], gd[1, 2, :, cs]), NN)

    o = [jnp.where(good, p, q) for p, q in ((zi + 2, hi + 1), (zi + 1, lo - 1), (zi - 1, hi), (zi, lo))]

    def shalf(s, h):
        return remote(
            half(x + 2, o[s], h), xh.at[s, h], ss_t.at[s, h], rs_t.at[s, h], xp if h == 0 else xm
        )

    def sfull(s, h):
        return remote(
            blk(x + 1 - 2 * h, o[s]), xf.at[s, h], ss_q.at[s, h], rs_q.at[s, h], xp if h == 0 else xm
        )

    def by(d, step, q, b, dst):
        return remote(
            chunk(b, q), dst.at[d, :, pl.ds(q * 512, 512)],
            ss_bz.at[d, step, q], rs_by.at[d, step, q], zm if d else zp,
        )

    def take(d, step, q, b, dst):
        by(d, step, q, b, dst).wait_recv()
        where = (2, rows(b), slice(q * 512, q * 512 + 512))
        wg[where] = wg[where] + dst[d, :, q * 512 : q * 512 + 512]

    weight_grad(x + 2)
    for s in range(4):
        for h in range(2):
            shalf(s, h).start()
    weight_grad_b(0)

    @pl.when(good)
    def _():
        by(0, 0, 0, zi + 2, y0).start()

    @pl.when(bad)
    def _():
        by(1, 0, 0, lo - 1, y1).start()

    weight_grad_b(1)

    @pl.when(good)
    def _():
        by(1, 0, 1, zi + 2, y0).start()

    @pl.when(bad)
    def _():
        by(0, 0, 1, hi + 1, y1).start()

    weight_grad(x + 1)
    weight_grad(x - 1)

    @pl.when(bad)
    def _():
        take(0, 0, 0, hi + 1, y0)
        by(0, 0, 0, hi + 1, y1).start()
        take(1, 0, 1, lo - 1, y0)
        by(1, 0, 1, lo - 1, y1).start()

    for s in range(4):
        for h in range(2):
            shalf(s, h).wait_recv()
            where = (slice(0, 2), rows(o[s]), hcols(x + 1 - 2 * h, h))
            wg[where] = wg[where] + xh[s, h]
            sfull(s, h).start()

    @pl.when(good)
    def _():
        take(0, 0, 1, zi + 1, y1)
        by(0, 1, 1, zi + 1, y2b).start()
        take(1, 0, 0, zi - 1, y1)
        by(1, 1, 0, zi - 1, y2b).start()

    weight_grad(x)

    @pl.when(good)
    def _():
        take(0, 0, 0, zi + 1, y1)
        by(0, 1, 0, zi + 1, y2b).start()
        take(1, 0, 1, zi - 1, y1)
        by(1, 1, 1, zi - 1, y2b).start()

    returns = []

    def token_grad(i):
        y2 = (y + STEPS[i]) % 4
        r = pl.ds(pl.multiple_of(y2 * 256, 256), 256)
        res = dot3((wsp[0, 0], wsp[1, 0]), (gd[0, 0, r, :], gd[1, 0, r, :]), NT)
        res = res + dot3((wsp[0, 1], wsp[1, 1]), (gd[0, 1, r, :], gd[1, 1, r, :]), NT)
        xs[y2 * 2, 0:448, :] = res[:, 0:128]
        xs[y2 * 2 + 1, 0:448, :] = res[:, 128:256]
        for n, (dc, dy) in enumerate(OTHERS):
            if dy == STEPS[i]:
                m = y2 * 2 + (c + dc) % 2
                cp = remote(
                    xs.at[m, pl.ds(0, 448), :], cg.at[me], ss_y.at[n], rs_y.at[n], dev(x, y2, z, c + dc)
                )
                cp.start()
                returns.append(cp)

    def total_x(s):
        sfull(s, 0).wait_recv()
        sfull(s, 1).wait_recv()
        where = (slice(0, 2), rows(o[s]), cols(x))
        wg[where] = wg[where] + xf[s, 0] + xf[s, 1]

    def add(s, v):
        where = (slice(0, 2), rows(o[s]), cols(x))
        wg[where] = wg[where] + v

    def add_half(s, h, v):
        where = (slice(0, 2), rows(o[s]), hcols(x, h))
        wg[where] = wg[where] + v

    def zs(i, src, dst):
        return remote(src, dst, ss_s.at[i], rs_s.at[i], zp if i < 2 else zm)

    def bh(h):
        return remote(bhalf(x + 2, h), yh.at[h], ss_bx.at[h], rs_by2.at[h], xm if h else xp)

    def bf(h):
        return remote(bblk(x + 1 - 2 * h), yf.at[h], ss_bx.at[2 + h], rs_by2.at[2 + h], xm if h else xp)

    total_x(0)

    @pl.when(good)
    def _():
        zs(0, half(x, o[0], 0), zh.at[0]).start()
        zs(2, half(x, o[0], 1), zh.at[1]).start()

    @pl.when(bad)
    def _():
        take(0, 1, 1, hi, y2b)
        by(0, 1, 1, hi, y3).start()
        take(1, 1, 0, lo, y2b)
        by(1, 1, 0, lo, y3).start()

    token_grad(0)
    token_grad(1)

    @pl.when(bad)
    def _():
        zs(0, half(x, o[0], 0), zh.at[0]).wait_recv()
        add_half(0, 0, zh[0])
        zs(0, blk(x, o[0]), z1.at[0]).start()

    total_x(1)

    @pl.when(bad)
    def _():
        zs(2, half(x, o[1], 1), zh.at[1]).wait_recv()
        add_half(1, 1, zh[1])
        zs(2, blk(x, o[1]), z1.at[1]).start()
        take(0, 1, 0, hi, y2b)
        by(0, 1, 0, hi, y3).start()
        take(1, 1, 1, lo, y2b)
        by(1, 1, 1, lo, y3).start()

    token_grad(2)
    token_grad(3)

    @pl.when(good)
    def _():
        zs(0, blk(x, o[1]), z1.at[0]).wait_recv()
        add(1, z1[0])
        zs(1, blk(x, o[1]), z2.at[0]).start()

    total_x(2)

    @pl.when(good)
    def _():
        zs(2, blk(x, o[2]), z1.at[1]).wait_recv()
        add(2, z1[1])
        zs(3, blk(x, o[2]), z2.at[1]).start()
        for q in (0, 1):
            take(0, 1, 1 - q, zi, y3)
            take(1, 1, q, zi, y3)
        bh(0).start()
        bh(1).start()

    @pl.when(bad)
    def _():
        zs(1, blk(x, o[2]), z2.at[0]).wait_recv()
        add(2, z2[0])
        zs(1, blk(x, o[2]), z3.at[0]).start()

    total_x(3)

    @pl.when(bad)
    def _():
        zs(3, blk(x, o[3]), z2.at[1]).wait_recv()
        add(3, z2[1])
        zs(3, blk(x, o[3]), z3.at[1]).start()

    @pl.when(good)
    def _():
        for h in range(2):
            bh(h).wait_recv()
            where = (2, rows(zi), hcols(x + 1 - 2 * h, h))
            wg[where] = wg[where] + yh[h]
            bf(h).start()

    cg[me] = xs[me, 0:448, :]

    for cp in returns:
        cp.wait()
    for j in range(28):
        t = jnp.concatenate([cg[m, to : to + n, :] for m, to, frm, n in PIECES[j]], axis=0)
        tokv[:, j * 128 : (j + 1) * 128] = t.T
    leave = pltpu.make_async_copy(tokv, out, s_l.at[5])
    leave.start()

    @pl.when(good)
    def _():
        bf(0).wait_recv()
        bf(1).wait_recv()
        where = (2, rows(zi), cols(x))
        wg[where] = wg[where] + yf[0] + yf[1]
        back_b = remote(bhalf(x, 1 - yl), gout.at[2], ss_p.at[1], rs_p.at[4], partner)
        back_b.start()
        zs(1, blk(x, o[3]), z3.at[0]).wait_recv()
        zs(3, blk(x, o[3]), z3.at[1]).wait_recv()
        add(3, z3[0] + z3[1])
        back = remote(half(x, zi, 1 - yl), gout.at[0:2], ss_p.at[0], rs_p.at[3], partner)
        back.start()
        gout[...] = wg[:, rows(zi), hcols(x, yl)]
        back.wait_send()
        back_b.wait_send()
        zs(0, half(x, o[0], 0), zh.at[0]).wait_send()
        zs(2, half(x, o[0], 1), zh.at[1]).wait_send()
        by(0, 0, 0, zi + 2, y0).wait_send()
        by(1, 0, 1, zi + 2, y0).wait_send()
        for h in range(2):
            bh(h).wait_send()
            bf(h).wait_send()

    @pl.when(bad)
    def _():
        remote(half(x, zi, 1 - yl), gout.at[0:2], ss_p.at[0], rs_p.at[3], partner).wait_recv()
        remote(bhalf(x, 1 - yl), gout.at[2], ss_p.at[1], rs_p.at[4], partner).wait_recv()
        zs(0, blk(x, o[0]), z1.at[0]).wait_send()
        zs(2, blk(x, o[1]), z1.at[1]).wait_send()
        for q in (0, 1):
            by(0, 0, q, hi + 1, y1).wait_send()
            by(1, 0, q, lo - 1, y1).wait_send()

    for q in (0, 1):
        by(0, 1, q, zi, y2b).wait_send()
        by(1, 1, q, zi, y2b).wait_send()
    zs(1, blk(x, o[2]), z3.at[0]).wait_send()
    zs(3, blk(x, o[3]), z3.at[1]).wait_send()
    leave.wait()
    for s in range(4):
        for h in range(2):
            shalf(s, h).wait_send()
            sfull(s, h).wait_send()


def local(tokens, cotangent, routes, gates, w_gate, w_up, w_down):
    vm = pl.BlockSpec(memory_space=pltpu.VMEM)
    anyspace = pl.BlockSpec(memory_space=pl.ANY)
    dma = pltpu.SemaphoreType.DMA
    full, hlf = (2, ROWS, 256), (2, ROWS, 128)

    def f32(*shape):
        return pltpu.VMEM(shape, F32)

    def bf16(*shape):
        return pltpu.VMEM(shape, BF16)

    out, gout = pl.pallas_call(
        kernel,
        out_shape=(jax.ShapeDtypeStruct((TOK, 3584), F32), jax.ShapeDtypeStruct((3, ROWS, 128), F32)),
        in_specs=[anyspace] * 2 + [vm] * 5,
        out_specs=(anyspace, vm),
        scratch_shapes=[
            f32(TOK, 3584), f32(TOK, 3584), f32(8, 456, TOK), f32(8, 448, TOK), f32(8, 456, TOK), f32(8, 448, TOK), f32(3, 448, 1024),
            bf16(2, 3, 448, 1024), bf16(2, 1024, 448), bf16(2, 256, 448), bf16(2, 2, 448, 1024), f32(8, TOK, 8), f32(4, 2, TOK, 768),
            f32(4, TOK, 768), f32(2, 64, 768), f32(2, TOK, 768), f32(4, 2, TOK, 768), bf16(2, 3, 1024, 1024),
            f32(4, 2, *hlf), f32(4, 2, *full),
            f32(2, *hlf), f32(2, *full), f32(2, *full), f32(2, *full),
            f32(2, ROWS, 1024), f32(2, ROWS, 1024), f32(2, ROWS, 1024), f32(2, ROWS, 1024),
            f32(2, ROWS, 128), f32(2, ROWS, 256),
            dma((4,)), dma((4,)), dma((2, 2, 2)), dma((2, 2, 2)), dma((2, 2, 2)), dma((4,)),
            dma((7,)), dma((7,)), dma((7,)), dma((7,)), dma((7,)), dma((4,)), dma((5,)), dma((4,)), dma((4,)),
            dma((4, 4)), dma((4, 4)),
            dma((2, 4)), dma((2, 4)), dma((2, 4)), dma((2, 4)), dma((4,)), dma((4,)), dma((4,)), dma((4,)),
            dma((4, 2)), dma((4, 2)), dma((4, 2)), dma((4, 2)), dma((7,)), dma((7,)), dma((4,)), dma((4,)),
        ],
        compiler_params=pltpu.CompilerParams(
            collective_id=0, has_side_effects=True, vmem_limit_bytes=VMEM_LIMIT
        ),
        cost_estimate=pl.CostEstimate(flops=20_000_000_000, bytes_accessed=8_000_000, transcendentals=40_000),
    )(tokens, cotangent, routes.T, gates.T, w_gate[0], w_up[0], w_down[0])
    return out, gout[0:1], gout[1:2], gout[2:3]


def solution(mesh):
    rows = P(("dp", "expert"), None)
    weights = P("expert", "dp", None)
    return jax.shard_map(
        local,
        mesh=mesh,
        in_specs=(rows, rows, rows, rows, weights, weights, weights),
        out_specs=(rows, weights, weights, weights),
        check_vma=False,
    )
```
